256 devices in a mesh: section: 16 (over z_hi, y, core), dp: 16 (over x, z_lo).
Axes of the slice: x: 4, y: 4, z: 8 (z_hi: 2, z_lo: 4; z = z_hi * 4 + z_lo), core: 2. Of those that a mesh axis runs over, the one named last changes fastest.
Arguments:
- handoff: bfloat16 [16, 4096, 2048], P('section', 'dp'), may hold values from -6 to 6
- memory_slot: bfloat16 [16, 4096, 2048], P('section', 'dp'), may hold values from -6 to 6
- memory_length: int32 [16, 16], P('section', 'dp'), may hold values from 32 to 256
- saved_input: bfloat16 [16, 4096, 2048], P('section', 'dp'), may hold values from -6 to 6
- saved_memory: bfloat16 [16, 4096, 2048], P('section', 'dp'), may hold values from -6 to 6
- saved_length: int32 [16, 16], P('section', 'dp'), may hold values from 32 to 256
- grad_handoff: bfloat16 [16, 4096, 2048], P('section', 'dp'), may hold values from -6 to 6
- memory_grad_partial: float32 [16, 4096, 2048], P('section', 'dp'), may hold values from -6 to 6
- section_weight: bfloat16 [16, 2048, 2048], P('section', 'dp'), may hold values from -40 to 40
- section_gain: float32 [16, 2048], P('section'), may hold values from 0.5 to 1.5
Outputs:
- section_output: bfloat16 [16, 4096, 2048], P('section', 'dp')
- input_grad: bfloat16 [16, 4096, 2048], P('section', 'dp')
- memory_grad: float32 [16, 4096, 2048], P('section', 'dp')
- weight_grad: float32 [16, 2048, 2048], P('section', 'dp')
- gain_grad: float32 [16, 2048], P('section', 'dp')
The draws below stay inside these ranges and needn't reach their ends.
All inputs are finite; a program needn't handle non-finite values.
Results may differ from the reference program's by a relative error of at most 0.033.
The reference program's roundings to bfloat16 on the way count: a program that leaves them out, or rounds other values in their place, can miss the bound.
Values may be sent and summed in bfloat16 or wider, within the bound.
No kernel may reach another device: no remote copies, remote signals or barrier semaphores. Data moves between devices by JAX's collectives and lax.ppermute only.
A program may use at most 192 MiB of HBM per device.

```python
import jax
import jax.numpy as jnp
from jax import lax

HEADS = 32
HEAD = 64
D = 2048
ROWS = 256
SECTIONS = 16
SEQ_ROWS = 4096
N_SECTION = 16
N_DP = 16


def paired_rows(key, offset):
    first = jnp.clip(jax.random.normal(jax.random.fold_in(key, offset), (SECTIONS, SEQ_ROWS, D), jnp.float32), -6.0, 6.0)
    second = jnp.clip(jax.random.normal(jax.random.fold_in(key, offset + 1), (SECTIONS, SEQ_ROWS, D), jnp.float32), -6.0, 6.0)
    return (first, second)


def draw_handoff(key, part):
    first, second = paired_rows(key, 11)
    return first.astype(jnp.bfloat16)


def draw_memory_slot(key, part):
    first, second = paired_rows(key, 11)
    return second.astype(jnp.bfloat16)


def draw_saved_input(key, part):
    first, second = paired_rows(key, 21)
    return first.astype(jnp.bfloat16)


def draw_saved_memory(key, part):
    first, second = paired_rows(key, 21)
    return second.astype(jnp.bfloat16)


def draw_section_weight(key, part):
    key = jax.random.fold_in(key, 7)
    noise = jnp.clip(jax.random.normal(key, (SECTIONS, D, D), jnp.float32), -6.0, 6.0)
    matrix = noise * D ** (-0.5)
    return matrix.astype(jnp.bfloat16)


def place_ends(entries, own_key, smallest, top_value):
    longest = entries.shape.index(max(entries.shape))
    spots = []
    for shift in (0, 1):
        where = [jax.random.randint(jax.random.fold_in(own_key, axis), (), 0, length) for axis, length in enumerate(entries.shape)]
        where[longest] = (where[longest] + shift) % entries.shape[longest]
        spots.append(tuple(where))
    return entries.at[spots[0]].set(smallest).at[spots[1]].set(top_value)


def block_levels(own_key, shape, pieces, smallest, largest):
    level, own = 1.0, jax.random.fold_in(own_key, 6)
    for dim, parts in pieces:
        steps = jnp.exp(jax.random.uniform(jax.random.fold_in(own, dim), (parts,), jnp.float32, smallest / len(pieces), largest / len(pieces)))
        level = level * jnp.repeat(steps, shape[dim] // parts).reshape([-1 if axis == dim else 1 for axis in range(len(shape))])
    return level


def scatter_about(rng, dims, width, limit, cuts=(), kind=jnp.bfloat16):
    gain = block_levels(rng, dims, cuts, -0.22, 0.18) if cuts else 1.0
    values = jax.random.normal(rng, dims, jnp.float32) * width * gain
    return jnp.minimum(jnp.maximum(values, -limit), limit).astype(kind)


def setup_inputs(seed: int = 0) -> dict:
    splits = jax.random.split(jax.random.key(seed), 11)
    return {
        "handoff": draw_handoff(jax.random.fold_in(splits[10], 71), 0),
        "memory_slot": draw_memory_slot(jax.random.fold_in(splits[10], 71), 0),
        "memory_length": place_ends(jax.random.randint(splits[2], (SECTIONS, N_DP), ROWS // 8, ROWS + 1), jax.random.fold_in(splits[2], 1), ROWS // 8, ROWS).astype(jnp.int32),
        "saved_input": draw_saved_input(jax.random.fold_in(splits[10], 71), 0),
        "saved_memory": draw_saved_memory(jax.random.fold_in(splits[10], 71), 0),
        "saved_length": place_ends(jax.random.randint(splits[5], (SECTIONS, N_DP), ROWS // 8, ROWS + 1), jax.random.fold_in(splits[5], 1), ROWS // 8, ROWS).astype(jnp.int32),
        "grad_handoff": scatter_about(splits[6], (SECTIONS, SEQ_ROWS, D), 1.0, 6.0, ((0, 16), (1, 16))),
        "memory_grad_partial": scatter_about(splits[7], (SECTIONS, SEQ_ROWS, D), 1.0, 6.0, ((0, 16), (1, 16)), jnp.float32),
        "section_weight": draw_section_weight(jax.random.fold_in(splits[10], 71), 0),
        "section_gain": jnp.clip(1.0 + 0.1 * jax.random.normal(splits[9], (SECTIONS, D), jnp.float32), 0.5, 1.5),
    }


epsilon = 1e-06

def normalize(values):
    values = values.astype(jnp.float32)
    inverse = lax.rsqrt(lax.optimization_barrier(jnp.mean(values * values, axis=-1, keepdims=True)) + epsilon)
    return (values * inverse, inverse)

def attend(queries, keys_bf, values, length):
    count = queries.shape[0]
    query_heads = queries.reshape(count, HEADS, HEAD)
    key_heads = keys_bf.reshape(count, HEADS, HEAD)
    value_heads = values.reshape(count, HEADS, HEAD)
    scores = jnp.einsum('qhd,khd->hqk', query_heads.astype(jnp.float32), key_heads.astype(jnp.float32)) * HEAD ** (-0.5)
    valid = jnp.arange(count, dtype=jnp.int32) < length
    scores = jnp.where(valid[None, None, :], scores, -1e+30)
    weights = jax.nn.softmax(scores, axis=-1)
    weights_bf = weights.astype(jnp.bfloat16)
    mixed = jnp.einsum('hqk,khd->qhd', weights_bf.astype(jnp.float32), value_heads.astype(jnp.float32))
    return (mixed.reshape(count, HEADS * HEAD), weights, weights_bf, query_heads, key_heads, value_heads)

def encode(inputs, weight, gain_vector):
    normed, inverse = normalize(inputs)
    projected = jnp.dot((normed * gain_vector).astype(jnp.bfloat16), weight, preferred_element_type=jnp.float32)
    return (inputs.astype(jnp.float32) + jax.nn.gelu(projected)).astype(jnp.bfloat16)

def decode(targets, memory, length, weight, gain_vector):
    normed, inverse = normalize(targets)
    queries = jnp.dot((normed * gain_vector).astype(jnp.bfloat16), weight, preferred_element_type=jnp.float32).astype(jnp.bfloat16)
    key_normed, key_inverse = normalize(memory)
    mixed = attend(queries, key_normed.astype(jnp.bfloat16), memory, length)[0]
    return (targets.astype(jnp.float32) + mixed).astype(jnp.bfloat16)

def norm_back(grad_normed, normed, inverse):
    return inverse * grad_normed - normed * inverse * lax.optimization_barrier(jnp.mean(grad_normed * normed, axis=-1, keepdims=True))

def encode_back(inputs, cotangent, weight, gain_vector):
    normed, inverse = normalize(inputs)
    lowered = (normed * gain_vector).astype(jnp.bfloat16)
    projected = jnp.dot(lowered, weight, preferred_element_type=jnp.float32)
    gelu_back = jax.vjp(jax.nn.gelu, projected)[1]
    grad_proj = gelu_back(cotangent)[0].astype(jnp.bfloat16)
    weight_term = jnp.dot(lowered.T, grad_proj, preferred_element_type=jnp.float32)
    grad_lowered = jnp.dot(grad_proj, weight.T, preferred_element_type=jnp.float32)
    gain_term = lax.optimization_barrier(jnp.sum(grad_lowered * normed, axis=0))
    grad_inputs = cotangent + norm_back(grad_lowered * gain_vector, normed, inverse)
    return (grad_inputs.astype(jnp.bfloat16), weight_term, gain_term, jnp.zeros_like(cotangent))

def decode_back(targets, memory, length, cotangent, carried, weight, gain_vector):
    count = targets.shape[0]
    normed, inverse = normalize(targets)
    lowered = (normed * gain_vector).astype(jnp.bfloat16)
    queries = jnp.dot(lowered, weight, preferred_element_type=jnp.float32).astype(jnp.bfloat16)
    key_normed, key_inverse = normalize(memory)
    keys_bf = key_normed.astype(jnp.bfloat16)
    mixed, weights, weights_bf, query_heads, key_heads, value_heads = attend(queries, keys_bf, memory, length)
    grad_heads = cotangent.astype(jnp.bfloat16).reshape(count, HEADS, HEAD).astype(jnp.float32)
    grad_weights = jnp.einsum('qhd,khd->hqk', grad_heads, value_heads.astype(jnp.float32))
    grad_scores = weights * (grad_weights - lax.optimization_barrier(jnp.sum(grad_weights * weights, axis=-1, keepdims=True)))
    grad_scores = (grad_scores * HEAD ** (-0.5)).astype(jnp.bfloat16).astype(jnp.float32)
    grad_queries = jnp.einsum('hqk,khd->qhd', grad_scores, key_heads.astype(jnp.float32)).reshape(count, HEADS * HEAD).astype(jnp.bfloat16)
    grad_keys = jnp.einsum('hqk,qhd->khd', grad_scores, query_heads.astype(jnp.float32)).reshape(count, HEADS * HEAD)
    grad_values = jnp.einsum('hqk,qhd->khd', weights_bf.astype(jnp.float32), grad_heads).reshape(count, HEADS * HEAD)
    memory_term = grad_values + norm_back(grad_keys, key_normed, key_inverse)
    weight_term = jnp.dot(lowered.T, grad_queries, preferred_element_type=jnp.float32)
    grad_lowered = jnp.dot(grad_queries, weight.T, preferred_element_type=jnp.float32)
    gain_term = lax.optimization_barrier(jnp.sum(grad_lowered * normed, axis=0))
    grad_inputs = cotangent + norm_back(grad_lowered * gain_vector, normed, inverse)
    return (grad_inputs.astype(jnp.bfloat16), weight_term, gain_term, memory_term + carried)

def reference(handoff, memory_slot, memory_length, saved_input, saved_memory, saved_length, grad_handoff, memory_grad_partial, section_weight, section_gain):
    encoder_count = N_SECTION // 2

    def split(array):
        return array.reshape(N_SECTION, N_DP, ROWS, D)
    prev_main = jnp.roll(split(handoff), 1, axis=0)
    prev_other = jnp.roll(split(memory_slot), 1, axis=0)
    prev_length = jnp.roll(memory_length, 1, axis=0)
    next_grad = jnp.roll(split(grad_handoff), -1, axis=0)
    next_partial = jnp.roll(split(memory_grad_partial), -1, axis=0)
    stored_input = split(saved_input)
    stored_memory = split(saved_memory)

    def per_section(section_index):
        weight = section_weight[section_index]
        gain_vector = section_gain[section_index]

        def per_replica(carry, replica):
            incoming = prev_main[section_index, replica]
            other_slot = prev_other[section_index, replica]
            length_in = prev_length[section_index, replica]
            upstream = next_grad[section_index, replica].astype(jnp.float32)
            partial_in = next_partial[section_index, replica]
            held_input = stored_input[section_index, replica]
            held_memory = stored_memory[section_index, replica]
            held_length = saved_length[section_index, replica]

            def run_decoder(unused):
                first_decoder = section_index == encoder_count
                targets = jnp.where(first_decoder, other_slot, incoming)
                memory = jnp.where(first_decoder, incoming, other_slot)
                output = decode(targets, memory, length_in, weight, gain_vector)
                carried = jnp.where(section_index == N_SECTION - 1, jnp.zeros_like(partial_in), partial_in)
                return (output,) + decode_back(held_input, held_memory, held_length, upstream, carried, weight, gain_vector)

            def run_encoder(unused):
                output = encode(incoming, weight, gain_vector)
                cotangent = jnp.where(section_index == encoder_count - 1, partial_in, upstream)
                return (output,) + encode_back(held_input, cotangent, weight, gain_vector)
            output, grad_inputs, weight_term, gain_term, memory_term = lax.cond(section_index >= encoder_count, run_decoder, run_encoder, 0)
            return ((carry[0] + weight_term, carry[1] + gain_term), (output, grad_inputs, memory_term))
        start = (jnp.zeros((D, D), jnp.float32), jnp.zeros((D,), jnp.float32))
        sums, rows_out = lax.scan(per_replica, start, jnp.arange(N_DP, dtype=jnp.int32))
        return (rows_out[0], rows_out[1], rows_out[2], sums[0], sums[1])
    outputs, grads, memory_terms, weight_sums, gain_sums = lax.map(per_section, jnp.arange(N_SECTION, dtype=jnp.int32))
    shape = (N_SECTION, N_DP * ROWS, D)
    return (outputs.reshape(shape), grads.reshape(shape), memory_terms.reshape(shape), weight_sums, gain_sums)
```

```python
import functools

import jax
import jax.numpy as jnp
from jax import lax
from jax.experimental import pallas as pl
from jax.experimental.pallas import tpu as pltpu
from jax.sharding import PartitionSpec as P

HEADS = 32
HEAD = 64
D = 2048
ROWS = 256
BF = jnp.bfloat16
F32 = jnp.float32
WIDTH = 512
CHUNKS = D // WIDTH
QUAD = 512

epsilon = 1e-06
GELU_A = 0.7978845608028654
GELU_B = 0.044715

NT = (((1,), (1,)), ((), ()))


def dot(a, b):
    return jnp.dot(a, b, preferred_element_type=F32)


def dot_nt(a, b):
    return lax.dot_general(a, b, NT, preferred_element_type=F32)


def rows_loop(count, step, body):
    def run(index, carry):
        body(pl.ds(pl.multiple_of(index * step, step), step))
        return carry

    lax.fori_loop(0, count // step, run, 0)


def norm_rows(values):
    values = values.astype(F32)
    inverse = lax.rsqrt(jnp.mean(values * values, axis=-1, keepdims=True) + epsilon)
    return values * inverse, inverse


def prologue_back(info, x_ref, m_ref, g_ref, u_ref, ut_ref, k_ref):
    def body(rows):
        normed, _ = norm_rows(x_ref[rows, :])
        u_ref[rows, :] = (normed * g_ref[...]).astype(BF)

    rows_loop(ROWS, 32, body)

    @pl.when(info[0] == 1)
    def _():
        def keys(rows):
            k_ref[rows, :] = norm_rows(m_ref[rows, :])[0].astype(BF)

        rows_loop(ROWS, 32, keys)

    for index in range(D // 256):
        cols = slice(index * 256, index * 256 + 256)
        ut_ref[cols, :] = u_ref[:, cols].T


def prologue_forward(info, h_ref, s_ref, g_ref, u_ref, k_ref):
    first = info[1] == 1

    def body(rows):
        y = jnp.where(first, s_ref[rows, :].astype(F32), h_ref[rows, :].astype(F32))
        u_ref[rows, :] = (norm_rows(y)[0] * g_ref[...]).astype(BF)

    rows_loop(ROWS, 32, body)

    @pl.when(info[0] == 1)
    def _():
        def keys(rows):
            m = jnp.where(first, h_ref[rows, :].astype(F32), s_ref[rows, :].astype(F32))
            k_ref[rows, :] = norm_rows(m)[0].astype(BF)

        rows_loop(ROWS, 32, keys)


def project(info, base, u_ref, s_ref, r_ref, z_ref):
    width = s_ref.shape[1]
    for tile in range(width // 256):
        cols = slice(tile * 256, tile * 256 + 256)
        total = None
        for index in range(4):
            part = s_ref if index < 2 else r_ref
            first = QUAD * (index % 2)
            place = pl.multiple_of(info[base + index] * QUAD, QUAD)
            term = dot(u_ref[:, pl.ds(place, QUAD)], part[first : first + QUAD, cols])
            total = term if total is None else total + term
        z_ref[:, cols] = total


def lane_masks():
    lane = lax.broadcasted_iota(jnp.int32, (ROWS, 128), 1)
    return lane < HEAD, lane >= HEAD


def softmax_parts(scores, length):
    column = lax.broadcasted_iota(jnp.int32, scores.shape, 1)
    scores = jnp.where(column < length, scores, -1e30)
    top = jnp.max(scores, axis=-1, keepdims=True)
    raised = jnp.exp(scores - top)
    return raised * (1.0 / jnp.sum(raised, axis=-1, keepdims=True))


def back_chunk(info, u_ref, ut_ref, s_ref, r_ref, c_ref, k_ref, v_ref, dz_ref, ds_ref, dr_ref, dk_ref, dv_ref, z_ref, *, base):
    project(info, base, u_ref, s_ref, r_ref, z_ref)

    @pl.when(info[0] == 0)
    def _():
        def body(rows):
            z = z_ref[rows, :]
            square = z * z
            t = jnp.tanh(GELU_A * (z + GELU_B * (square * z)))
            slope = 0.5 * (1.0 + t) + (0.5 * GELU_A) * z * (1.0 - t * t) * (1.0 + (3 * GELU_B) * square)
            dz_ref[rows, :] = (c_ref[rows, :].astype(F32) * slope).astype(BF)

        rows_loop(ROWS, 32, body)

    @pl.when(info[0] == 1)
    def _():
        length = info[2]

        def pair(index, carry):
            cols = pl.ds(pl.multiple_of(index * 128, 128), 128)
            q = z_ref[:, cols].astype(BF)
            k = k_ref[:, cols]
            v = v_ref[:, cols]
            do = c_ref[:, cols]
            qt = q.T
            dot_t = do.T
            q_small = (q.astype(F32) * 0.125).astype(BF)
            do_small = (do.astype(F32) * 0.125).astype(BF)
            zero = jnp.zeros((), BF)
            total = None
            dks, dvs = [], []
            for head, mask in enumerate(lane_masks()):
                p = softmax_parts(dot_nt(jnp.where(mask, q_small, zero), k), length)
                dp = dot_nt(jnp.where(mask, do_small, zero), v)
                shift = jnp.sum(dp * p, axis=-1, keepdims=True)
                ds = (p * (dp - shift)).astype(BF)
                pb = p.astype(BF)
                term = dot(ds, jnp.where(mask, k, zero))
                total = term if total is None else total + term
                rows = slice(head * HEAD, head * HEAD + HEAD)
                dks.append(dot(qt[rows, :], ds))
                dvs.append(dot(dot_t[rows, :], pb))
            dz_ref[:, cols] = total.astype(BF)
            dk_ref[:, cols] = jnp.concatenate(dks, axis=0).T
            dv_ref[:, cols] = jnp.concatenate(dvs, axis=0).T
            return carry

        lax.fori_loop(0, WIDTH // 128, pair, 0)

    for index in range(4):
        out = ds_ref if index < 2 else dr_ref
        first = QUAD * (index % 2)
        place = pl.multiple_of(info[base + index] * QUAD, QUAD)
        for tile in range(WIDTH // 256):
            cols = slice(tile * 256, tile * 256 + 256)
            out[first : first + QUAD, cols] = dot(ut_ref[pl.ds(place, QUAD), :], dz_ref[:, cols]).astype(BF)


def forward_chunk(info, u_ref, s_ref, r_ref, h_ref, m_ref, k_ref, old_ref, out_ref, z_ref, *, base):
    project(info, base, u_ref, s_ref, r_ref, z_ref)

    @pl.when(info[0] == 0)
    def _():
        def body(rows):
            z = z_ref[rows, :]
            t = jnp.tanh(GELU_A * (z + GELU_B * (z * z * z)))
            out_ref[rows, :] = (h_ref[rows, :].astype(F32) + 0.5 * z * (1.0 + t)).astype(BF)

        rows_loop(ROWS, 32, body)

    @pl.when(info[0] == 1)
    def _():
        length = info[3]
        first = info[1] == 1

        def pair(index, carry):
            cols = pl.ds(pl.multiple_of(index * 128, 128), 128)
            q = (z_ref[:, cols].astype(BF).astype(F32) * 0.125).astype(BF)
            k = k_ref[:, cols]
            h = h_ref[:, cols].astype(F32)
            m = m_ref[:, cols].astype(F32)
            y = jnp.where(first, m, h)
            v = jnp.where(first, h, m).astype(BF)
            zero = jnp.zeros((), BF)
            total = y
            for mask in lane_masks():
                p = softmax_parts(dot_nt(jnp.where(mask, q, zero), k), length)
                total = total + dot(p.astype(BF), jnp.where(mask, v, zero))
            out_ref[:, cols] = total.astype(BF)
            return carry

        lax.fori_loop(0, WIDTH // 128, pair, 0)


def epilogue(info, *refs):
    dzs, refs = refs[:CHUNKS], refs[CHUNKS:]
    parts, refs = refs[: 2 * CHUNKS], refs[2 * CHUNKS :]
    dks, refs = refs[:CHUNKS], refs[CHUNKS:]
    dvs, refs = refs[:CHUNKS], refs[CHUNKS:]
    x_ref, c_ref, m_ref, a_ref, g_ref, dx_ref, dg_ref, dm_ref, du_ref = refs
    for chunk in range(CHUNKS):
        base = 4 + 4 * (chunk % 2)
        for index in range(4):
            part = parts[2 * chunk + index // 2]
            first = QUAD * (index % 2)
            place = pl.multiple_of(info[base + index] * QUAD, QUAD)
            cols = pl.ds(place, QUAD)
            term = dot_nt(dzs[chunk][...], part[first : first + QUAD, :])
            if chunk == 0:
                du_ref[:, cols] = term
            else:
                du_ref[:, cols] += term
    dg_ref[...] = jnp.zeros_like(dg_ref)

    def body(rows):
        normed, inverse = norm_rows(x_ref[rows, :])
        du = du_ref[rows, :]
        dg_ref[...] += jnp.sum(du * normed, axis=0, keepdims=True)
        h = du * g_ref[...]
        mean = jnp.mean(h * normed, axis=-1, keepdims=True)
        dx_ref[rows, :] = (c_ref[rows, :].astype(F32) + inverse * h - normed * (inverse * mean)).astype(BF)

    rows_loop(ROWS, 32, body)

    @pl.when(info[0] == 0)
    def _():
        dm_ref[...] = jnp.zeros_like(dm_ref)

    @pl.when(info[0] == 1)
    def _():
        def back(rows):
            normed, inverse = norm_rows(m_ref[rows, :])
            dk = jnp.concatenate([ref[rows, :] for ref in dks], axis=1)
            dv = jnp.concatenate([ref[rows, :] for ref in dvs], axis=1)
            mean = jnp.mean(dk * normed, axis=-1, keepdims=True)
            dm_ref[rows, :] = dv + inverse * dk - normed * (inverse * mean) + a_ref[rows, :].astype(F32)

        rows_loop(ROWS, 32, back)


def call(body, info, ins, outs, scratch=(), aliases=None, flops=0, limit=48, name=None):
    def spec(shape, block):
        if block == -1:
            return pl.BlockSpec(memory_space=pl.ANY)
        if block is None:
            return pl.BlockSpec(shape, lambda step, info: (0,) * len(shape))
        return pl.BlockSpec((shape[0], WIDTH), lambda step, info: (0, block))

    size = sum(2 * a.size for a, b in ins if b != -1)
    return pl.pallas_call(
        body,
        grid_spec=pltpu.PrefetchScalarGridSpec(
            num_scalar_prefetch=1,
            grid=(1,),
            in_specs=[spec(a.shape, b) for a, b in ins],
            out_specs=[spec(s, b) for s, _, b in outs],
            scratch_shapes=list(scratch),
        ),
        out_shape=[jax.ShapeDtypeStruct(s, t) for s, t, _ in outs],
        input_output_aliases=aliases or {},
        compiler_params=pltpu.CompilerParams(vmem_limit_bytes=limit * 2**20),
        cost_estimate=pl.CostEstimate(flops=flops, bytes_accessed=size, transcendentals=0),
        name=name,
    )(info, *[a for a, _ in ins])


def dp_permute(value, step):
    pairs = []
    for x in range(4):
        for z in range(4):
            to = step(x, z)
            if to is not None:
                pairs.append((x * 4 + z, to[0] * 4 + to[1]))
    return lax.ppermute(value, "dp", pairs)


def z_swap(x, z):
    return (x, z ^ 1)


def z_middle(x, z):
    return (x, 3 - z) if z in (1, 2) else None


def z_outward(x, z):
    return {1: (x, 0), 2: (x, 3)}.get(z)


def z_inward(x, z):
    return {0: (x, 1), 3: (x, 2)}.get(z)


def x_swap(x, z):
    return (x ^ 1, z)


def x_cross(x, z):
    return (3 - x, z)


def gather_pair(shard, z):
    odd = z % 2 == 1
    high = z >= 2
    outer = (z == 0) | (z == 3)
    other = dp_permute(shard, z_swap)
    pair = jnp.concatenate([jnp.where(odd, other, shard), jnp.where(odd, shard, other)], axis=0)
    inner = dp_permute(pair, z_middle)
    last = dp_permute(inner, z_outward)
    rest = jnp.where(outer, last, inner)
    quad = jnp.concatenate([jnp.where(high, rest, pair), jnp.where(high, pair, rest)], axis=0)
    half = shard.shape[1] // 2
    out = []
    for part, first, second in ((quad[:, :half], x_swap, x_cross), (quad[:, half:], x_cross, x_swap)):
        near = jnp.concatenate([part, dp_permute(part, first)], axis=0)
        out.append((near, dp_permute(near, second)))
    return out


def add(a, b):
    return (a.astype(F32) + b.astype(F32)).astype(BF)


def reduce_pair(terms, z):
    odd = z % 2 == 1
    high = z >= 2
    quads = []
    for (near, far), first, second in ((terms[0], x_cross, x_swap), (terms[1], x_swap, x_cross)):
        came = dp_permute(far, first)
        away = add(near[QUAD:], came[QUAD:])
        back = dp_permute(away, second)
        quads.append((near[:QUAD].astype(F32) + came[:QUAD].astype(F32) + back.astype(F32)).astype(BF))
    quad = jnp.concatenate(quads, axis=1)
    other = jnp.where(high, quad[:256], quad[256:])
    mine = jnp.where(high, quad[256:], quad[:256])
    inward = dp_permute(other, z_inward)
    crossed = dp_permute(add(other, inward), z_middle)
    mine = add(mine, crossed)
    kept = jnp.where(odd, mine[128:], mine[:128])
    given = jnp.where(odd, mine[:128], mine[128:])
    return kept.astype(F32) + dp_permute(given, z_swap).astype(F32)


def on_device(
    handoff,
    memory_slot,
    memory_length,
    saved_input,
    saved_memory,
    saved_length,
    grad_handoff,
    memory_grad_partial,
    section_weight,
    section_gain,
):
    section = lax.axis_index("section")
    replica = lax.axis_index("dp")
    count = lax.axis_size("section")
    half = count // 2
    x, z = replica // 4, replica % 4
    gain = section_gain
    shard = section_weight[0]

    def along(value, pairs):
        return lax.ppermute(value, "section", pairs)

    chunks = []
    for pair in range(CHUNKS // 2):
        chunks += gather_pair(shard[:, pair * 2 * WIDTH : (pair + 1) * 2 * WIDTH], z)

    partial = memory_grad_partial[0].astype(BF)
    upstream = jnp.where(section == half, partial, grad_handoff[0])
    cotangent = along(upstream, [(s, (s - 1) % count) for s in range(count)])
    carried = along(partial, [(s, s - 1) for s in range(half + 1, count)])
    incoming = along(handoff[0], [(s, (s + 1) % count) for s in range(count)])
    slot = along(memory_slot[0], [(s, s + 1) for s in range(half - 1, count - 1)])
    length = along(memory_length[0], [(s, s + 1) for s in range(half - 1, count - 1)])

    swap, cross = x + 1 - 2 * (x % 2), 3 - x
    far = cross + 1 - 2 * (cross % 2)
    is_decoder = (section >= half).astype(jnp.int32)
    is_first = (section == half).astype(jnp.int32)
    head = [is_decoder, is_first, saved_length[0, 0]]
    order = [x, swap, cross, far, x, cross, swap, far]
    zero = jnp.int32(0)
    info_back = jnp.stack([v.astype(jnp.int32) for v in head + [zero] + order])
    info_forward = jnp.stack([v.astype(jnp.int32) for v in head + [length[0]] + order])

    whole = lambda t: ((ROWS, D), t, None)
    u_back, ut_back, k_back = call(
        prologue_back,
        info_back,
        [(saved_input[0], None), (saved_memory[0], None), (gain, None)],
        [whole(BF), ((D, ROWS), BF, None), whole(BF)],
        flops=10**9,
        name="prologue_back",
    )
    back = []
    for index, (near, other) in enumerate(chunks):
        part = ((ROWS, WIDTH), F32, None)
        rows = ((1024, WIDTH), BF, None)
        back.append(
            call(
                functools.partial(back_chunk, base=4 + 4 * (index % 2)),
                info_back,
                [
                    (u_back, None),
                    (ut_back, None),
                    (near, None),
                    (other, None),
                    (cotangent, index),
                    (k_back, index),
                    (saved_memory[0], index),
                ],
                [((ROWS, WIDTH), BF, None), rows, rows, part, part],
                scratch=[pltpu.VMEM((ROWS, WIDTH), F32)],
                flops=8 * 10**9,
                name="back_chunk",
            )
        )
    sums = []
    for pair in range(CHUNKS // 2):
        sums.append(reduce_pair([back[2 * pair + i][1:3] for i in (0, 1)], z))
    weight_sum = jnp.concatenate(sums, axis=1)

    u_forward, k_forward = call(
        prologue_forward,
        info_forward,
        [(incoming, None), (slot, None), (gain, None)],
        [whole(BF), whole(BF)],
        flops=10**9,
        name="prologue_forward",
    )
    result = u_forward
    for index, (near, other) in enumerate(chunks):
        old = [(result, -1)] if index else []
        (result,) = call(
            functools.partial(forward_chunk if index else forward_first, base=4 + 4 * (index % 2)),
            info_forward,
            [(u_forward, None), (near, None), (other, None), (incoming, index), (slot, index), (k_forward, index)] + old,
            [((ROWS, D), BF, index)],
            scratch=[pltpu.VMEM((ROWS, WIDTH), F32)],
            aliases={7: 0} if index else None,
            flops=5 * 10**9,
            name="forward_chunk",
        )

    grad_input, gain_term, memory_term = call(
        epilogue,
        info_back,
        [(b[0], None) for b in back]
        + [(part, None) for both in chunks for part in both]
        + [(b[3], None) for b in back]
        + [(b[4], None) for b in back]
        + [(saved_input[0], None), (cotangent, None), (saved_memory[0], None), (carried, None), (gain, None)],
        [whole(BF), ((1, D), F32, None), whole(F32)],
        scratch=[pltpu.VMEM((ROWS, D), F32)],
        flops=5 * 10**9,
        limit=60,
        name="epilogue",
    )
    gain_sum = lax.psum_scatter(gain_term[0], "dp", scatter_dimension=0, tiled=True)
    return result[None], grad_input[None], memory_term[None], weight_sum[None], gain_sum[None]


def forward_first(info, u_ref, s_ref, r_ref, h_ref, m_ref, k_ref, out_ref, z_ref, *, base):
    forward_chunk(info, u_ref, s_ref, r_ref, h_ref, m_ref, k_ref, None, out_ref, z_ref, base=base)


def solution(mesh):
    rows = P("section", "dp", None)
    one = P("section", "dp")
    return jax.shard_map(
        on_device,
        mesh=mesh,
        in_specs=(rows, rows, one, rows, rows, one, rows, rows, rows, P("section", None)),
        out_specs=(rows, rows, rows, rows, one),
        check_vma=False,
    )
```

```python
import functools

import jax
import jax.numpy as jnp
from jax import lax
from jax.experimental import pallas as pl
from jax.experimental.pallas import tpu as pltpu
from jax.sharding import PartitionSpec as P

HEADS = 32
HEAD = 64
D = 2048
ROWS = 256
BF = jnp.bfloat16
F32 = jnp.float32
PAIRS = (256, 512, 256)
CHUNKS = 2 * len(PAIRS)
QUAD = 512

epsilon = 1e-06
GELU_A = 0.7978845608028654
GELU_B = 0.044715

NT = (((1,), (1,)), ((), ()))


def dot(a, b):
    return jnp.dot(a, b, preferred_element_type=F32)


def dot_nt(a, b):
    return lax.dot_general(a, b, NT, preferred_element_type=F32)


def rows_loop(count, step, body):
    def run(index, carry):
        body(pl.ds(pl.multiple_of(index * step, step), step))
        return carry

    lax.fori_loop(0, count // step, run, 0)


def add(a, b):
    return (a.astype(F32) + b.astype(F32)).astype(BF)


def norm_rows(values):
    values = values.astype(F32)
    inverse = lax.rsqrt(jnp.mean(values * values, axis=-1, keepdims=True) + epsilon)
    return values * inverse, inverse


def prologue_back(info, x_ref, m_ref, g_ref, u_ref, ut_ref, k_ref):
    def body(rows):
        normed, _ = norm_rows(x_ref[rows, :])
        u_ref[rows, :] = (normed * g_ref[...]).astype(BF)

    rows_loop(ROWS, 32, body)

    @pl.when(info[0] == 1)
    def _():
        def keys(rows):
            k_ref[rows, :] = norm_rows(m_ref[rows, :])[0].astype(BF)

        rows_loop(ROWS, 32, keys)

    for index in range(D // 256):
        cols = slice(index * 256, index * 256 + 256)
        ut_ref[cols, :] = u_ref[:, cols].T


def prologue_forward(info, h_ref, s_ref, g_ref, u_ref, k_ref):
    first = info[1] == 1

    def body(rows):
        y = jnp.where(first, s_ref[rows, :].astype(F32), h_ref[rows, :].astype(F32))
        u_ref[rows, :] = (norm_rows(y)[0] * g_ref[...]).astype(BF)

    rows_loop(ROWS, 32, body)

    @pl.when(info[0] == 1)
    def _():
        def keys(rows):
            m = jnp.where(first, h_ref[rows, :].astype(F32), s_ref[rows, :].astype(F32))
            k_ref[rows, :] = norm_rows(m)[0].astype(BF)

        rows_loop(ROWS, 32, keys)


def gathered(info, source, quad):
    return jnp.concatenate([source[:, pl.ds(block_place(info, quad, i), 128)] for i in range(4)], axis=1)


def block_place(info, quad, index):
    return pl.multiple_of(info[4 + 4 * quad + index] * 128, 128)


def project(info, u_ref, parts, z_ref):
    width = z_ref.shape[1]
    for tile in range(width // 256):
        cols = slice(tile * 256, tile * 256 + 256)
        total = None
        for quad, part in enumerate(parts):
            term = dot(gathered(info, u_ref, quad), part[:, cols])
            total = term if total is None else total + term
        z_ref[:, cols] = total


def lane_masks():
    lane = lax.broadcasted_iota(jnp.int32, (ROWS, 128), 1)
    return lane < HEAD, lane >= HEAD


def softmax_parts(scores, length):
    column = lax.broadcasted_iota(jnp.int32, scores.shape, 1).astype(F32)
    scores = jnp.where(column < length, scores, -1e30)
    top = jnp.max(scores, axis=-1, keepdims=True)
    raised = jnp.exp(scores - top)
    return raised * (1.0 / jnp.sum(raised, axis=-1, keepdims=True))


def back_chunk(info, u_ref, ut_ref, w0, w1, w2, w3, c_ref, k_ref, v_ref, dz_ref, d0, d1, d2, d3, dk_ref, dv_ref, z_ref):
    project(info, u_ref, (w0, w1, w2, w3), z_ref)

    @pl.when(info[0] == 0)
    def _():
        def body(rows):
            z = z_ref[rows, :]
            square = z * z
            t = jnp.tanh(GELU_A * (z + GELU_B * (square * z)))
            slope = 0.5 * (1.0 + t) + (0.5 * GELU_A) * z * (1.0 - t * t) * (1.0 + (3 * GELU_B) * square)
            dz_ref[rows, :] = (c_ref[rows, :].astype(F32) * slope).astype(BF)

        rows_loop(ROWS, 32, body)

    @pl.when(info[0] == 1)
    def _():
        length = info[2].astype(F32)

        def pair(index, carry):
            cols = pl.ds(pl.multiple_of(index * 128, 128), 128)
            q = z_ref[:, cols].astype(BF)
            k = k_ref[:, cols]
            v = v_ref[:, cols]
            do = c_ref[:, cols]
            qt = q.T
            dot_t = do.T
            q_small = (q.astype(F32) * 0.125).astype(BF)
            do_small = (do.astype(F32) * 0.125).astype(BF)
            zero = jnp.zeros((), BF)
            total = None
            dks, dvs = [], []
            for head, mask in enumerate(lane_masks()):
                p = softmax_parts(dot_nt(jnp.where(mask, q_small, zero), k), length)
                dp = dot_nt(jnp.where(mask, do_small, zero), v)
                shift = jnp.sum(dp * p, axis=-1, keepdims=True)
                ds = (p * (dp - shift)).astype(BF)
                pb = p.astype(BF)
                term = dot(ds, jnp.where(mask, k, zero))
                total = term if total is None else total + term
                rows = slice(head * HEAD, head * HEAD + HEAD)
                dks.append(dot(qt[rows, :], ds))
                dvs.append(dot(dot_t[rows, :], pb))
            dz_ref[:, cols] = total.astype(BF)
            dk_ref[:, cols] = jnp.concatenate(dks, axis=0).T
            dv_ref[:, cols] = jnp.concatenate(dvs, axis=0).T
            return carry

        lax.fori_loop(0, z_ref.shape[1] // 128, pair, 0)

    for quad, out in enumerate((d0, d1, d2, d3)):
        ut = jnp.concatenate([ut_ref[pl.ds(block_place(info, quad, i), 128), :] for i in range(4)], axis=0)
        for tile in range(z_ref.shape[1] // 256):
            cols = slice(tile * 256, tile * 256 + 256)
            out[:, cols] = dot(ut, dz_ref[:, cols]).astype(BF)


def forward_chunk(info, u_ref, w0, w1, w2, w3, h_ref, m_ref, k_ref, n_ref, old_ref, out_ref, z_ref):
    project(info, u_ref, (w0, w1, w2, w3), z_ref)

    @pl.when(info[0] == 0)
    def _():
        def body(rows):
            z = z_ref[rows, :]
            t = jnp.tanh(GELU_A * (z + GELU_B * (z * z * z)))
            out_ref[rows, :] = (h_ref[rows, :].astype(F32) + 0.5 * z * (1.0 + t)).astype(BF)

        rows_loop(ROWS, 32, body)

    @pl.when(info[0] == 1)
    def _():
        length = n_ref[...].astype(F32)[:1, :1]
        first = info[1] == 1

        def pair(index, carry):
            cols = pl.ds(pl.multiple_of(index * 128, 128), 128)
            q = (z_ref[:, cols].astype(BF).astype(F32) * 0.125).astype(BF)
            k = k_ref[:, cols]
            h = h_ref[:, cols].astype(F32)
            m = m_ref[:, cols].astype(F32)
            y = jnp.where(first, m, h)
            v = jnp.where(first, h, m).astype(BF)
            zero = jnp.zeros((), BF)
            total = y
            for mask in lane_masks():
                p = softmax_parts(dot_nt(jnp.where(mask, q, zero), k), length)
                total = total + dot(p.astype(BF), jnp.where(mask, v, zero))
            out_ref[:, cols] = total.astype(BF)
            return carry

        lax.fori_loop(0, z_ref.shape[1] // 128, pair, 0)


def epilogue(info, *refs):
    dzs, refs = refs[:CHUNKS], refs[CHUNKS:]
    parts, refs = refs[: 4 * CHUNKS], refs[4 * CHUNKS :]
    dks, refs = refs[:CHUNKS], refs[CHUNKS:]
    dvs, refs = refs[:CHUNKS], refs[CHUNKS:]
    cs, refs = refs[:2], refs[2:]
    x_ref, m_ref, a_ref, g_ref, dx_ref, dm_ref, du_ref = refs
    for quad in range(4):
        total = None
        for chunk in range(CHUNKS):
            term = dot_nt(dzs[chunk][...], parts[4 * chunk + quad][...])
            total = term if total is None else total + term
        for index in range(4):
            du_ref[:, pl.ds(block_place(info, quad, index), 128)] = total[:, index * 128 : index * 128 + 128]

    def body(rows):
        normed, inverse = norm_rows(x_ref[rows, :])
        du = du_ref[rows, :]
        h = du * g_ref[...]
        mean = jnp.mean(h * normed, axis=-1, keepdims=True)
        c = jnp.concatenate([ref[rows, :] for ref in cs], axis=1).astype(F32)
        dx_ref[rows, :] = (c + inverse * h - normed * (inverse * mean)).astype(BF)

    rows_loop(ROWS, 32, body)

    @pl.when(info[0] == 0)
    def _():
        dm_ref[...] = jnp.zeros_like(dm_ref)

    @pl.when(info[0] == 1)
    def _():
        def back(rows):
            normed, inverse = norm_rows(m_ref[rows, :])
            dk = jnp.concatenate([ref[rows, :] for ref in dks], axis=1)
            dv = jnp.concatenate([ref[rows, :] for ref in dvs], axis=1)
            mean = jnp.mean(dk * normed, axis=-1, keepdims=True)
            dm_ref[rows, :] = dv + inverse * dk - normed * (inverse * mean) + a_ref[rows, :].astype(F32)

        rows_loop(ROWS, 32, back)


def extend_rows(info, value, out):
    out[:ROWS, :] = value[...]
    out[ROWS:, :] = jnp.full((16, D), info[3].astype(F32), F32).astype(BF)


def split_columns(info, value, *outs):
    start = 0
    for out in outs:
        out[...] = value[:, start : start + out.shape[1]]
        start += out.shape[1]


def cotangent_kernel(info, p_ref, g_ref, up0, up1, pb_ref):
    first = info[1] == 1

    def body(rows):
        p = p_ref[rows, :]
        pb_ref[rows, :] = p.astype(BF)
        up = jnp.where(first, p, g_ref[rows, :].astype(F32)).astype(BF)
        up0[rows, :] = up[:, : up0.shape[1]]
        up1[rows, :] = up[:, up0.shape[1] :]

    rows_loop(ROWS, 32, body)


def stack_rows(info, *refs):
    parts, outs = refs[:4], refs[4:]
    for index, part in enumerate(parts):
        start = 0
        for out in outs:
            out[index * 128 : index * 128 + 128, :] = part[:, start : start + out.shape[1]]
            start += out.shape[1]


def take_two(info, one, two, out_one, out_two):
    out_one[...] = one[...]
    out_two[...] = two[...]


def first_sums(info, q1a, sa, q1b, q2a, q2b, sb, one, two):
    width = q1a.shape[1]
    one[:, :width] = add(q1a[...], sa[...])
    one[:, width:] = q1b[...]
    two[:, :width] = q2a[...]
    two[:, width:] = add(q2b[...], sb[...])


def second_sums(info, own_a, own_b, t1, t2, keep, s1, s2, s3):
    width = own_a.shape[1]
    for index, out in enumerate((keep, s1, s2, s3)):
        rows = slice(index * 128, index * 128 + 128)
        for own, cols in ((own_a, slice(0, width)), (own_b, slice(width, 2 * width))):
            total = own[rows, :].astype(F32) + t1[rows, cols].astype(F32) + t2[rows, cols].astype(F32)
            out[:, cols] = total.astype(out.dtype)


def half_sums(info, own_a, own_b, t1, t2, keep, sent):
    width = own_a.shape[1]
    for own, cols in ((own_a, slice(0, width)), (own_b, slice(width, 2 * width))):
        total = own[...].astype(F32) + t1[:, cols].astype(F32) + t2[:, cols].astype(F32)
        keep[:, cols] = total[:256]
        sent[:, cols] = total[256:].astype(BF)


def quarter_sums(info, kept, came, keep, sent):
    total = kept[...] + came[...].astype(F32)
    keep[...] = total[:128]
    sent[...] = total[128:].astype(BF)


def last_sums(info, *refs):
    w_ref, g_ref, out_ref, gain_ref = refs[-4:]
    total = None
    start = 0
    for p in range(len(PAIRS)):
        some = 4 if p == 1 else 2
        (keep, *came), refs = refs[:some], refs[some:]
        value = keep[...]
        for part in came:
            value += part[...].astype(F32)
        cols = slice(start, start + keep.shape[1])
        start += keep.shape[1]
        out_ref[:, cols] = value
        term = jnp.sum(value * w_ref[:, cols].astype(F32), axis=1, keepdims=True)
        total = term if total is None else total + term
    gain_ref[...] = jnp.broadcast_to(total, (128, 128)).T[0:1, :] / g_ref[...]


def call(body, info, ins, outs, scratch=(), aliases=None, flops=1, limit=20, name=None):
    def spec(shape, block):
        if block == -1:
            return pl.BlockSpec(memory_space=pl.ANY)
        if block == "length":
            return pl.BlockSpec((16, 128), lambda step, info: (ROWS // 16, 0))
        if block == "rows":
            return pl.BlockSpec((ROWS, D), lambda step, info: (0, 0))
        if block is None:
            return pl.BlockSpec(shape, lambda step, info: (0,) * len(shape))
        start, width = block
        return pl.BlockSpec((ROWS if shape[0] == ROWS + 16 else shape[0], width), lambda step, info: (0, start // width))

    return pl.pallas_call(
        body,
        grid_spec=pltpu.PrefetchScalarGridSpec(
            num_scalar_prefetch=1,
            grid=(1,),
            in_specs=[spec(a.shape, b) for a, b in ins],
            out_specs=[spec(s, b) for s, _, b in outs],
            scratch_shapes=list(scratch),
        ),
        out_shape=[jax.ShapeDtypeStruct(s, t) for s, t, _ in outs],
        input_output_aliases=aliases or {},
        compiler_params=pltpu.CompilerParams(vmem_limit_bytes=limit * 2**20),
        cost_estimate=pl.CostEstimate(flops=flops, bytes_accessed=1, transcendentals=0),
        name=name,
    )(info, *[a for a, _ in ins])


def dp_permute(value, step):
    pairs = []
    for x in range(4):
        for z in range(4):
            to = step(x, z)
            if to is not None:
                pairs.append((x * 4 + z, to[0] * 4 + to[1]))
    return lax.ppermute(value, "dp", pairs)


def z_steps(value):
    return [dp_permute(value, functools.partial(z_to, step)) for step in (1, 2, 3)]


def z_two(total):
    return dp_permute(total, functools.partial(z_to, 2))


def z_to(step, x, z):
    return (x, z ^ step)


def x_swap(x, z):
    return (x ^ 1, z)


def x_cross(x, z):
    return (3 - x, z)


def tie(value, *after):
    return lax.optimization_barrier((value, *after))[0] if after else value


def on_device(
    handoff,
    memory_slot,
    memory_length,
    saved_input,
    saved_memory,
    saved_length,
    grad_handoff,
    memory_grad_partial,
    section_weight,
    section_gain,
):
    section = lax.axis_index("section")
    replica = lax.axis_index("dp")
    count = lax.axis_size("section")
    half = count // 2
    x, z = replica // 4, replica % 4
    gain = section_gain
    shard = section_weight[0]

    def along(value, pairs):
        return lax.ppermute(value, "section", pairs)

    starts = [0]
    for width in PAIRS:
        starts.append(starts[-1] + 2 * width)
    blocks = [(starts[i] + h * w, w) for i, w in enumerate(PAIRS) for h in (0, 1)]
    marks = []

    def first(value):
        return tie(value, *marks)

    def mark(value):
        marks[:] = [value]
        return value

    count_pairs = len(PAIRS)
    quads, near, far = {}, {}, {}
    is_decoder = (section >= half).astype(jnp.int32)
    is_first = (section == half).astype(jnp.int32)
    order = [(x ^ i) * 4 + (z ^ j) for i in (0, 1, 3, 2) for j in range(4)]

    lengths = [saved_length[0, 0], memory_length[0, 0]]
    info = jnp.stack([v.astype(jnp.int32) for v in [is_decoder, is_first] + lengths + order])

    def small(body, ins, shapes, name):
        ins = [i if isinstance(i, tuple) else (i, None) for i in ins]
        ins[0] = (first(ins[0][0]), ins[0][1])
        out = call(body, info, ins, [(*shape, None) for shape in shapes], name=name)
        mark(out[0])
        return out

    head = 2 * PAIRS[0]
    columns = ((128, head), BF), ((128, D - head), BF)
    shard_a, shard_b = small(split_columns, [shard], columns, "split")
    came_a = z_steps(shard_a)
    upstream_a, upstream_b, partial = small(
        cotangent_kernel,
        [memory_grad_partial[0], grad_handoff[0]],
        [((ROWS, head), BF), ((ROWS, D - head), BF), ((ROWS, D), BF)],
        "cotangent",
    )
    cotangents = {}

    def send_cotangent(part, pairs):
        part = along(first(part), [(s, (s - 1) % count) for s in range(count)])
        for index in pairs:
            cotangents[index] = (part, starts[index] - starts[pairs[0]])

    send_cotangent(upstream_a, [0])

    def send_x(p):
        sent = first(quads[p])
        near[p] = (dp_permute(sent, x_swap), dp_permute(sent, x_cross))

    def forward_x(p):
        w = PAIRS[p]
        one, two = small(take_two, [(near[p][0], (0, w)), (near[p][1], (w, w))], [((QUAD, w), BF)] * 2, "forward")
        far[p] = (dp_permute(one, x_cross), dp_permute(two, x_swap))

    def weights(p, kind):
        w = PAIRS[p]
        return [(a, (kind * w, w)) for a in (quads[p], *near[p])] + [(far[p][kind], None)]

    whole = lambda t: ((ROWS, D), t, None)
    u_back, ut_back, k_back = call(
        prologue_back,
        info,
        [(first(saved_input[0]), None), (saved_memory[0], None), (gain, None)],
        [whole(BF), ((D, ROWS), BF, None), whole(BF)],
        name="prologue_back",
    )
    mark(u_back)
    back, back_terms, sums = {}, {}, {}

    def back_work(p, kind):
        index = 2 * p + kind
        start, width = blocks[index]
        part = ((ROWS, width), F32, None)
        rows = ((QUAD, width), BF, None)
        out = call(
            back_chunk,
            info,
            [(first(u_back), None), (ut_back, None)]
            + weights(p, kind)
            + [(cotangents[p][0], (cotangents[p][1] + kind * width, width))]
            + [(a, blocks[index]) for a in (k_back, saved_memory[0])],
            [((ROWS, width), BF, None), rows, rows, rows, rows, part, part],
            scratch=[pltpu.VMEM((ROWS, width), F32)],
            name="back_chunk",
        )
        mark(out[0])
        back[index] = (out[0], out[5], out[6])
        back_terms[index] = list(out[1:5]) + [dp_permute(out[4], x_swap if kind else x_cross)]

    def reduce_first(p):
        a, b = back_terms[2 * p], back_terms[2 * p + 1]
        shape = ((QUAD, 2 * PAIRS[p]), BF)
        one, two = small(first_sums, [a[1], a[4], b[1], a[2], b[2], b[4]], [shape, shape], "first_sums")
        sums[p] = (dp_permute(one, x_swap), dp_permute(two, x_cross))

    def reduce_second(p):
        width = 2 * PAIRS[p]
        shapes = [((128, width), F32)] + [((128, width), BF)] * 3
        own = [back_terms[2 * p][0], back_terms[2 * p + 1][0]]
        keep, *sent = small(second_sums, own + list(sums[p]), shapes, "second_sums")
        sums[p] = [keep] + [dp_permute(part, functools.partial(z_to, i + 1)) for i, part in enumerate(sent)]

    def reduce_half(p):
        width = 2 * PAIRS[p]
        own = [back_terms[2 * p][0], back_terms[2 * p + 1][0]]
        keep, sent = small(half_sums, own + list(sums[p]), [((256, width), F32), ((256, width), BF)], "half_sums")
        sums[p] = [keep, z_two(sent)]

    def reduce_quarter(p):
        width = 2 * PAIRS[p]
        keep, sent = small(quarter_sums, sums[p], [((128, width), F32), ((128, width), BF)], "quarter_sums")
        sums[p] = [keep, dp_permute(sent, functools.partial(z_to, 1))]

    state = {}

    def send_incoming():
        state["incoming"] = along(first(handoff[0]), [(s, (s + 1) % count) for s in range(count)])

    def send_slot():
        (slot,) = small(extend_rows, [memory_slot[0]], [((ROWS + 16, D), BF)], "extend")
        state["slot"] = along(slot, [(s, s + 1) for s in range(half - 1, count - 1)])

    def send_carried():
        state["carried"] = along(first(partial), [(s, s - 1) for s in range(half + 1, count)])

    def wait(*values):
        marks.extend(values)

    def forward_start():
        state["u"], state["k"] = call(
            prologue_forward,
            info,
            [(first(state["incoming"]), None), (state["slot"], "rows"), (gain, None)],
            [whole(BF), whole(BF)],
            name="prologue_forward",
        )
        mark(state["u"])

    def forward_work(p, kind):
        index = 2 * p + kind
        old = [(state["result"], -1)] if "result" in state else []
        (state["result"],) = call(
            forward_chunk if old else forward_first,
            info,
            [(first(state["u"]), None)]
            + weights(p, kind)
            + [(a, blocks[index]) for a in (state["incoming"], state["slot"], state["k"])]
            + [(state["slot"], "length")]
            + old,
            [((ROWS, D), BF, blocks[index])],
            scratch=[pltpu.VMEM((ROWS, blocks[index][1]), F32)],
            aliases={10: 0} if old else None,
            name="forward_chunk",
        )
        mark(state["result"])

    def finish():
        kinds = [(p, k) for p in range(count_pairs) for k in (0, 1)]
        state["dx"], state["dm"] = call(
            epilogue,
            info,
            [(first(back[0][0]), None)]
            + [(back[i][0], None) for i in range(1, CHUNKS)]
            + [part for p, k in kinds for part in weights(p, k)]
            + [(back[i][1], None) for i in range(CHUNKS)]
            + [(back[i][2], None) for i in range(CHUNKS)]
            + [(cotangents[0][0], None), (cotangents[1][0], None)]
            + [(saved_input[0], None), (saved_memory[0], None), (state["carried"], None), (gain, None)],
            [whole(BF), whole(F32)],
            scratch=[pltpu.VMEM((ROWS, D), F32)],
            limit=44,
            name="epilogue",
        )
        mark(state["dx"])

    wait(cotangents[0][0])
    (quads[0],) = small(stack_rows, [shard_a] + came_a, [((QUAD, head), BF)], "stack")
    send_x(0)
    came_b = z_steps(first(shard_b))
    forward_x(0)
    back_work(0, 0)
    back_work(0, 1)
    quads[1], quads[2] = small(stack_rows, [shard_b] + came_b, [((QUAD, 2 * w), BF) for w in PAIRS[1:]], "stack")
    send_x(1)
    send_cotangent(upstream_b, [1, 2])
    reduce_first(0)
    forward_x(1)
    wait(cotangents[1][0])
    send_incoming()
    reduce_half(0)
    wait(*far[1])
    send_x(2)
    back_work(1, 0)
    forward_x(2)
    wait(state["incoming"])
    reduce_quarter(0)
    wait(*far[2])
    send_slot()
    wait(sums[0][1])
    back_work(1, 1)
    back_work(2, 0)
    back_work(2, 1)
    reduce_first(1)
    wait(state["slot"])
    send_carried()
    forward_start()
    forward_work(0, 0)
    forward_work(0, 1)
    forward_work(1, 0)
    reduce_first(2)
    forward_work(1, 1)
    forward_work(2, 0)
    forward_work(2, 1)
    reduce_second(1)
    finish()
    reduce_half(2)
    reduce_quarter(2)
    own_gain = lax.dynamic_slice_in_dim(gain, replica * 128, 128, axis=1)
    weight_sum, gain_sum = small(
        last_sums,
        [part for p in range(count_pairs) for part in sums[p]] + [shard, own_gain],
        [((128, D), F32), ((1, 128), F32)],
        "last_sums",
    )
    result, grad_input, memory_term = state["result"], state["dx"], state["dm"]
    return result[None], grad_input[None], memory_term[None], weight_sum[None], gain_sum


def forward_first(info, *refs):
    forward_chunk(info, *refs[:-2], None, *refs[-2:])


def solution(mesh):
    rows = P("section", "dp", None)
    one = P("section", "dp")
    return jax.shard_map(
        on_device,
        mesh=mesh,
        in_specs=(rows, rows, one, rows, rows, one, rows, rows, rows, P("section", None)),
        out_specs=(rows, rows, rows, rows, one),
        check_vma=False,
    )
```

```python
import functools

import jax
import jax.numpy as jnp
from jax import lax
from jax.experimental import pallas as pl
from jax.experimental.pallas import tpu as pltpu
from jax.sharding import PartitionSpec as P

HEADS = 32
HEAD = 64
D = 2048
ROWS = 256
BF = jnp.bfloat16
F32 = jnp.float32
PAIRS = (384, 384, 256)
CHUNKS = 2 * len(PAIRS)
QUAD = 512

epsilon = 1e-06
GELU_A = 0.7978845608028654
GELU_B = 0.044715

NT = (((1,), (1,)), ((), ()))


def dot(a, b):
    return jnp.dot(a, b, preferred_element_type=F32)


def dot_nt(a, b):
    return lax.dot_general(a, b, NT, preferred_element_type=F32)


def rows_loop(count, step, body):
    def run(index, carry):
        body(pl.ds(pl.multiple_of(index * step, step), step))
        return carry

    lax.fori_loop(0, count // step, run, 0)


def add(a, b):
    return (a.astype(F32) + b.astype(F32)).astype(BF)


def norm_rows(values):
    values = values.astype(F32)
    inverse = lax.rsqrt(jnp.mean(values * values, axis=-1, keepdims=True) + epsilon)
    return values * inverse, inverse


def prologue_back(info, x_ref, m_ref, g_ref, u_ref, ut_ref, k_ref):
    def body(rows):
        normed, _ = norm_rows(x_ref[rows, :])
        u_ref[rows, :] = (normed * g_ref[...]).astype(BF)

    rows_loop(ROWS, 32, body)

    @pl.when(info[0] == 1)
    def _():
        def keys(rows):
            k_ref[rows, :] = norm_rows(m_ref[rows, :])[0].astype(BF)

        rows_loop(ROWS, 32, keys)

    for index in range(D // 256):
        cols = slice(index * 256, index * 256 + 256)
        ut_ref[cols, :] = u_ref[:, cols].T


def prologue_forward(info, h_ref, s_ref, g_ref, u_ref, k_ref):
    first = info[1] == 1

    def body(rows):
        y = jnp.where(first, s_ref[rows, :].astype(F32), h_ref[rows, :].astype(F32))
        u_ref[rows, :] = (norm_rows(y)[0] * g_ref[...]).astype(BF)

    rows_loop(ROWS, 32, body)

    @pl.when(info[0] == 1)
    def _():
        def keys(rows):
            m = jnp.where(first, h_ref[rows, :].astype(F32), s_ref[rows, :].astype(F32))
            k_ref[rows, :] = norm_rows(m)[0].astype(BF)

        rows_loop(ROWS, 32, keys)


def gathered(info, source, quad):
    return jnp.concatenate([source[:, pl.ds(block_place(info, quad, i), 128)] for i in range(4)], axis=1)


def block_place(info, quad, index):
    return pl.multiple_of(info[4 + 4 * quad + index] * 128, 128)


def column_tiles(width):
    return [slice(start, min(start + 256, width)) for start in range(0, width, 256)]


def project(info, u_ref, parts, z_ref):
    width = z_ref.shape[1]
    for cols in column_tiles(width):
        total = None
        for quad, part in enumerate(parts):
            term = dot(gathered(info, u_ref, quad), part[:, cols])
            total = term if total is None else total + term
        z_ref[:, cols] = total


def lane_masks():
    lane = lax.broadcasted_iota(jnp.int32, (ROWS, 128), 1)
    return lane < HEAD, lane >= HEAD


def softmax_parts(scores, length):
    column = lax.broadcasted_iota(jnp.int32, scores.shape, 1).astype(F32)
    scores = jnp.where(column < length, scores, -1e30)
    top = jnp.max(scores, axis=-1, keepdims=True)
    raised = jnp.exp(scores - top)
    return raised * (1.0 / jnp.sum(raised, axis=-1, keepdims=True))


def back_chunk(info, u_ref, ut_ref, w0, w1, w2, w3, c_ref, k_ref, v_ref, dz_ref, d0, d1, d2, d3, dk_ref, dv_ref, z_ref):
    project(info, u_ref, (w0, w1, w2, w3), z_ref)

    @pl.when(info[0] == 0)
    def _():
        def body(rows):
            z = z_ref[rows, :]
            square = z * z
            t = jnp.tanh(GELU_A * (z + GELU_B * (square * z)))
            slope = 0.5 * (1.0 + t) + (0.5 * GELU_A) * z * (1.0 - t * t) * (1.0 + (3 * GELU_B) * square)
            dz_ref[rows, :] = (c_ref[rows, :].astype(F32) * slope).astype(BF)

        rows_loop(ROWS, 32, body)

    @pl.when(info[0] == 1)
    def _():
        length = info[2].astype(F32)

        def pair(index, carry):
            cols = pl.ds(pl.multiple_of(index * 128, 128), 128)
            q = z_ref[:, cols].astype(BF)
            k = k_ref[:, cols]
            v = v_ref[:, cols]
            do = c_ref[:, cols]
            qt = q.T
            dot_t = do.T
            q_small = (q.astype(F32) * 0.125).astype(BF)
            do_small = (do.astype(F32) * 0.125).astype(BF)
            zero = jnp.zeros((), BF)
            total = None
            dks, dvs = [], []
            for head, mask in enumerate(lane_masks()):
                p = softmax_parts(dot_nt(jnp.where(mask, q_small, zero), k), length)
                dp = dot_nt(jnp.where(mask, do_small, zero), v)
                shift = jnp.sum(dp * p, axis=-1, keepdims=True)
                ds = (p * (dp - shift)).astype(BF)
                pb = p.astype(BF)
                term = dot(ds, jnp.where(mask, k, zero))
                total = term if total is None else total + term
                rows = slice(head * HEAD, head * HEAD + HEAD)
                dks.append(dot(qt[rows, :], ds))
                dvs.append(dot(dot_t[rows, :], pb))
            dz_ref[:, cols] = total.astype(BF)
            dk_ref[:, cols] = jnp.concatenate(dks, axis=0).T
            dv_ref[:, cols] = jnp.concatenate(dvs, axis=0).T
            return carry

        lax.fori_loop(0, z_ref.shape[1] // 128, pair, 0)

    for quad, out in enumerate((d0, d1, d2, d3)):
        ut = jnp.concatenate([ut_ref[pl.ds(block_place(info, quad, i), 128), :] for i in range(4)], axis=0)
        for cols in column_tiles(z_ref.shape[1]):
            out[:, cols] = dot(ut, dz_ref[:, cols]).astype(BF)


def forward_chunk(info, u_ref, w0, w1, w2, w3, h_ref, m_ref, k_ref, n_ref, old_ref, out_ref, z_ref):
    project(info, u_ref, (w0, w1, w2, w3), z_ref)

    @pl.when(info[0] == 0)
    def _():
        def body(rows):
            z = z_ref[rows, :]
            t = jnp.tanh(GELU_A * (z + GELU_B * (z * z * z)))
            out_ref[rows, :] = (h_ref[rows, :].astype(F32) + 0.5 * z * (1.0 + t)).astype(BF)

        rows_loop(ROWS, 32, body)

    @pl.when(info[0] == 1)
    def _():
        length = n_ref[...].astype(F32)[:1, :1]
        first = info[1] == 1

        def pair(index, carry):
            cols = pl.ds(pl.multiple_of(index * 128, 128), 128)
            q = (z_ref[:, cols].astype(BF).astype(F32) * 0.125).astype(BF)
            k = k_ref[:, cols]
            h = h_ref[:, cols].astype(F32)
            m = m_ref[:, cols].astype(F32)
            y = jnp.where(first, m, h)
            v = jnp.where(first, h, m).astype(BF)
            zero = jnp.zeros((), BF)
            total = y
            for mask in lane_masks():
                p = softmax_parts(dot_nt(jnp.where(mask, q, zero), k), length)
                total = total + dot(p.astype(BF), jnp.where(mask, v, zero))
            out_ref[:, cols] = total.astype(BF)
            return carry

        lax.fori_loop(0, z_ref.shape[1] // 128, pair, 0)


def epilogue(info, *refs):
    dzs, refs = refs[:CHUNKS], refs[CHUNKS:]
    parts, refs = refs[: 4 * CHUNKS], refs[4 * CHUNKS :]
    dks, refs = refs[:CHUNKS], refs[CHUNKS:]
    dvs, refs = refs[:CHUNKS], refs[CHUNKS:]
    cs, refs = refs[:2], refs[2:]
    x_ref, m_ref, a_ref, g_ref, dx_ref, dm_ref, du_ref = refs
    for quad in range(4):
        total = None
        for chunk in range(CHUNKS):
            term = dot_nt(dzs[chunk][...], parts[4 * chunk + quad][...])
            total = term if total is None else total + term
        for index in range(4):
            du_ref[:, pl.ds(block_place(info, quad, index), 128)] = total[:, index * 128 : index * 128 + 128]

    def body(rows):
        normed, inverse = norm_rows(x_ref[rows, :])
        du = du_ref[rows, :]
        h = du * g_ref[...]
        mean = jnp.mean(h * normed, axis=-1, keepdims=True)
        c = jnp.concatenate([ref[rows, :] for ref in cs], axis=1).astype(F32)
        dx_ref[rows, :] = (c + inverse * h - normed * (inverse * mean)).astype(BF)

    rows_loop(ROWS, 32, body)

    @pl.when(info[0] == 0)
    def _():
        dm_ref[...] = jnp.zeros_like(dm_ref)

    @pl.when(info[0] == 1)
    def _():
        def back(rows):
            normed, inverse = norm_rows(m_ref[rows, :])
            dk = jnp.concatenate([ref[rows, :] for ref in dks], axis=1)
            dv = jnp.concatenate([ref[rows, :] for ref in dvs], axis=1)
            mean = jnp.mean(dk * normed, axis=-1, keepdims=True)
            dm_ref[rows, :] = dv + inverse * dk - normed * (inverse * mean) + a_ref[rows, :].astype(F32)

        rows_loop(ROWS, 32, back)


def extend_rows(info, value, out):
    out[:ROWS, :] = value[...]
    out[ROWS:, :] = jnp.full((16, D), info[3].astype(F32), F32).astype(BF)


def split_columns(info, value, *outs):
    start = 0
    for out in outs:
        out[...] = value[:, start : start + out.shape[1]]
        start += out.shape[1]


def cotangent_kernel(info, p_ref, g_ref, up0, up1, pb_ref):
    first = info[1] == 1

    def body(rows):
        p = p_ref[rows, :]
        pb_ref[rows, :] = p.astype(BF)
        up = jnp.where(first, p, g_ref[rows, :].astype(F32)).astype(BF)
        up0[rows, :] = up[:, : up0.shape[1]]
        up1[rows, :] = up[:, up0.shape[1] :]

    rows_loop(ROWS, 32, body)


def stack_rows(info, *refs):
    parts, outs = refs[:4], refs[4:]
    for index, part in enumerate(parts):
        start = 0
        for out in outs:
            out[index * 128 : index * 128 + 128, :] = part[:, start : start + out.shape[1]]
            start += out.shape[1]


def stack_two(info, one, two, *outs):
    start = 0
    for out in outs:
        cols = slice(start, start + out.shape[1])
        out[:128, :] = one[:, cols]
        out[128:, :] = two[:, cols]
        start += out.shape[1]


def stack_quad(info, one, two, out):
    out[:256, :] = one[...]
    out[256:, :] = two[...]


def take_two(info, one, two, out_one, out_two):
    out_one[...] = one[...]
    out_two[...] = two[...]


def first_sums(info, q1a, sa, q1b, q2a, q2b, sb, one, two):
    width = q1a.shape[1]
    one[:, :width] = add(q1a[...], sa[...])
    one[:, width:] = q1b[...]
    two[:, :width] = q2a[...]
    two[:, width:] = add(q2b[...], sb[...])


def second_sums(info, own_a, own_b, t1, t2, keep, s1, s2, s3):
    width = own_a.shape[1]
    for index, out in enumerate((keep, s1, s2, s3)):
        rows = slice(index * 128, index * 128 + 128)
        for own, cols in ((own_a, slice(0, width)), (own_b, slice(width, 2 * width))):
            total = own[rows, :].astype(F32) + t1[rows, cols].astype(F32) + t2[rows, cols].astype(F32)
            out[:, cols] = total.astype(out.dtype)


def half_sums(info, own_a, own_b, t1, t2, keep, sent):
    width = own_a.shape[1]
    for own, cols in ((own_a, slice(0, width)), (own_b, slice(width, 2 * width))):
        total = own[...].astype(F32) + t1[:, cols].astype(F32) + t2[:, cols].astype(F32)
        keep[:, cols] = total[:256]
        sent[:, cols] = total[256:].astype(BF)


def quarter_sums(info, kept, came, keep, sent):
    total = kept[...] + came[...].astype(F32)
    keep[...] = total[:128]
    sent[...] = total[128:].astype(BF)


def last_sums(info, *refs):
    w_ref, g_ref, out_ref, gain_ref = refs[-4:]
    total = None
    start = 0
    for p in range(len(PAIRS)):
        some = 4 if p == 1 else 2
        (keep, *came), refs = refs[:some], refs[some:]
        value = keep[...]
        for part in came:
            value += part[...].astype(F32)
        cols = slice(start, start + keep.shape[1])
        start += keep.shape[1]
        out_ref[:, cols] = value
        term = jnp.sum(value * w_ref[:, cols].astype(F32), axis=1, keepdims=True)
        total = term if total is None else total + term
    gain_ref[...] = jnp.broadcast_to(total, (128, 128)).T[0:1, :] / g_ref[...]


def call(body, info, ins, outs, scratch=(), aliases=None, flops=1, limit=20, name=None):
    def spec(shape, block):
        if block == -1:
            return pl.BlockSpec(memory_space=pl.ANY)
        if block == "length":
            return pl.BlockSpec((16, 128), lambda step, info: (ROWS // 16, 0))
        if block == "rows":
            return pl.BlockSpec((ROWS, D), lambda step, info: (0, 0))
        if block is None:
            return pl.BlockSpec(shape, lambda step, info: (0,) * len(shape))
        start, width = block
        return pl.BlockSpec((ROWS if shape[0] == ROWS + 16 else shape[0], width), lambda step, info: (0, start // width))

    return pl.pallas_call(
        body,
        grid_spec=pltpu.PrefetchScalarGridSpec(
            num_scalar_prefetch=1,
            grid=(1,),
            in_specs=[spec(a.shape, b) for a, b in ins],
            out_specs=[spec(s, b) for s, _, b in outs],
            scratch_shapes=list(scratch),
        ),
        out_shape=[jax.ShapeDtypeStruct(s, t) for s, t, _ in outs],
        input_output_aliases=aliases or {},
        compiler_params=pltpu.CompilerParams(vmem_limit_bytes=limit * 2**20),
        cost_estimate=pl.CostEstimate(flops=flops, bytes_accessed=1, transcendentals=0),
        name=name,
    )(info, *[a for a, _ in ins])


def dp_permute(value, step):
    pairs = []
    for x in range(4):
        for z in range(4):
            to = step(x, z)
            if to is not None:
                pairs.append((x * 4 + z, to[0] * 4 + to[1]))
    return lax.ppermute(value, "dp", pairs)


def z_steps(value):
    return [dp_permute(value, functools.partial(z_to, step)) for step in (1, 2, 3)]


def z_two(total):
    return dp_permute(total, functools.partial(z_to, 2))


def z_to(step, x, z):
    return (x, z ^ step)


def x_swap(x, z):
    return (x ^ 1, z)


def x_cross(x, z):
    return (3 - x, z)


def tie(value, *after):
    return lax.optimization_barrier((value, *after))[0] if after else value


def on_device(
    handoff,
    memory_slot,
    memory_length,
    saved_input,
    saved_memory,
    saved_length,
    grad_handoff,
    memory_grad_partial,
    section_weight,
    section_gain,
):
    section = lax.axis_index("section")
    replica = lax.axis_index("dp")
    count = lax.axis_size("section")
    half = count // 2
    x, z = replica // 4, replica % 4
    gain = section_gain
    shard = section_weight[0]

    def along(value, pairs):
        return lax.ppermute(value, "section", pairs)

    starts = [0]
    for width in PAIRS:
        starts.append(starts[-1] + 2 * width)
    blocks = [(starts[i] + h * w, w) for i, w in enumerate(PAIRS) for h in (0, 1)]
    marks = []

    def first(value):
        return tie(value, *marks)

    def mark(value):
        marks[:] = [value]
        return value

    count_pairs = len(PAIRS)
    quads, near, far = {}, {}, {}
    is_decoder = (section >= half).astype(jnp.int32)
    is_first = (section == half).astype(jnp.int32)
    order = [(x ^ i) * 4 + (z ^ j) for i in (0, 1, 3, 2) for j in range(4)]

    lengths = [saved_length[0, 0], memory_length[0, 0]]
    info = jnp.stack([v.astype(jnp.int32) for v in [is_decoder, is_first] + lengths + order])

    def small(body, ins, shapes, name):
        ins = [i if isinstance(i, tuple) else (i, None) for i in ins]
        ins[0] = (first(ins[0][0]), ins[0][1])
        out = call(body, info, ins, [(*shape, None) for shape in shapes], name=name)
        mark(out[0])
        return out

    head = 2 * PAIRS[0]
    columns = ((128, head), BF), ((128, D - head), BF)
    shard_a, shard_b = small(split_columns, [shard], columns, "split")
    came_a = z_steps(shard_a)
    swapped_b = dp_permute(shard_b, functools.partial(z_to, 1))
    upstream_a, upstream_b, partial = small(
        cotangent_kernel,
        [memory_grad_partial[0], grad_handoff[0]],
        [((ROWS, head), BF), ((ROWS, D - head), BF), ((ROWS, D), BF)],
        "cotangent",
    )
    cotangents = {}

    def send_cotangent(part, pairs):
        part = along(first(part), [(s, (s - 1) % count) for s in range(count)])
        for index in pairs:
            cotangents[index] = (part, starts[index] - starts[pairs[0]])

    def send_x(p):
        sent = first(quads[p])
        near[p] = (dp_permute(sent, x_swap), dp_permute(sent, x_cross))

    def forward_x(p):
        w = PAIRS[p]
        one, two = small(take_two, [(near[p][0], (0, w)), (near[p][1], (w, w))], [((QUAD, w), BF)] * 2, "forward")
        far[p] = (dp_permute(one, x_cross), dp_permute(two, x_swap))

    def weights(p, kind):
        w = PAIRS[p]
        return [(a, (kind * w, w)) for a in (quads[p], *near[p])] + [(far[p][kind], None)]

    whole = lambda t: ((ROWS, D), t, None)
    u_back, ut_back, k_back = call(
        prologue_back,
        info,
        [(first(saved_input[0]), None), (saved_memory[0], None), (gain, None)],
        [whole(BF), ((D, ROWS), BF, None), whole(BF)],
        name="prologue_back",
    )
    mark(u_back)
    back, back_terms, sums = {}, {}, {}

    def back_work(p, kind):
        index = 2 * p + kind
        start, width = blocks[index]
        part = ((ROWS, width), F32, None)
        rows = ((QUAD, width), BF, None)
        out = call(
            back_chunk,
            info,
            [(first(u_back), None), (ut_back, None)]
            + weights(p, kind)
            + [(cotangents[p][0], (cotangents[p][1] + kind * width, width))]
            + [(a, blocks[index]) for a in (k_back, saved_memory[0])],
            [((ROWS, width), BF, None), rows, rows, rows, rows, part, part],
            scratch=[pltpu.VMEM((ROWS, width), F32)],
            name="back_chunk",
        )
        mark(out[0])
        back[index] = (out[0], out[5], out[6])
        back_terms[index] = list(out[1:5]) + [dp_permute(out[4], x_swap if kind else x_cross)]

    def reduce_first(p):
        a, b = back_terms[2 * p], back_terms[2 * p + 1]
        shape = ((QUAD, 2 * PAIRS[p]), BF)
        one, two = small(first_sums, [a[1], a[4], b[1], a[2], b[2], b[4]], [shape, shape], "first_sums")
        sums[p] = (dp_permute(one, x_swap), dp_permute(two, x_cross))

    def reduce_second(p):
        width = 2 * PAIRS[p]
        shapes = [((128, width), F32)] + [((128, width), BF)] * 3
        own = [back_terms[2 * p][0], back_terms[2 * p + 1][0]]
        keep, *sent = small(second_sums, own + list(sums[p]), shapes, "second_sums")
        sums[p] = [keep] + [dp_permute(part, functools.partial(z_to, i + 1)) for i, part in enumerate(sent)]

    def reduce_half(p):
        width = 2 * PAIRS[p]
        own = [back_terms[2 * p][0], back_terms[2 * p + 1][0]]
        sums[p] = small(half_sums, own + list(sums[p]), [((256, width), F32), ((256, width), BF)], "half_sums")

    def send_half(p):
        sums[p] = [sums[p][0], z_two(first(sums[p][1]))]

    def reduce_quarter(p):
        width = 2 * PAIRS[p]
        keep, sent = small(quarter_sums, sums[p], [((128, width), F32), ((128, width), BF)], "quarter_sums")
        sums[p] = [keep, dp_permute(sent, functools.partial(z_to, 1))]

    state = {}

    def send_incoming():
        state["incoming"] = along(first(handoff[0]), [(s, (s + 1) % count) for s in range(count)])

    def make_slot():
        (state["extended"],) = small(extend_rows, [memory_slot[0]], [((ROWS + 16, D), BF)], "extend")

    def send_slot():
        state["slot"] = along(first(state["extended"]), [(s, s + 1) for s in range(half - 1, count - 1)])

    def send_carried():
        state["carried"] = along(first(partial), [(s, s - 1) for s in range(half + 1, count)])

    def wait(*values):
        marks.extend(values)

    def forward_start():
        state["u"], state["k"] = call(
            prologue_forward,
            info,
            [(first(state["incoming"]), None), (state["slot"], "rows"), (gain, None)],
            [whole(BF), whole(BF)],
            name="prologue_forward",
        )
        mark(state["u"])

    def forward_work(p, kind):
        index = 2 * p + kind
        old = [(state["result"], -1)] if "result" in state else []
        (state["result"],) = call(
            forward_chunk if old else forward_first,
            info,
            [(first(state["u"]), None)]
            + weights(p, kind)
            + [(a, blocks[index]) for a in (state["incoming"], state["slot"], state["k"])]
            + [(state["slot"], "length")]
            + old,
            [((ROWS, D), BF, blocks[index])],
            scratch=[pltpu.VMEM((ROWS, blocks[index][1]), F32)],
            aliases={10: 0} if old else None,
            name="forward_chunk",
        )
        mark(state["result"])

    def finish():
        kinds = [(p, k) for p in range(count_pairs) for k in (0, 1)]
        state["dx"], state["dm"] = call(
            epilogue,
            info,
            [(first(back[0][0]), None)]
            + [(back[i][0], None) for i in range(1, CHUNKS)]
            + [part for p, k in kinds for part in weights(p, k)]
            + [(back[i][1], None) for i in range(CHUNKS)]
            + [(back[i][2], None) for i in range(CHUNKS)]
            + [(cotangents[0][0], None), (cotangents[1][0], None)]
            + [(saved_input[0], None), (saved_memory[0], None), (state["carried"], None), (gain, None)],
            [whole(BF), whole(F32)],
            scratch=[pltpu.VMEM((ROWS, D), F32)],
            limit=44,
            name="epilogue",
        )
        mark(state["dx"])

    send_cotangent(upstream_a, [0])
    make_slot()
    halves = small(stack_two, [shard_b, swapped_b], [((256, 2 * w), BF) for w in PAIRS[1:]], "stack_two")
    rest_one = dp_permute(halves[0], functools.partial(z_to, 2))
    (quads[0],) = small(stack_rows, [shard_a] + came_a, [((QUAD, head), BF)], "stack")
    send_x(0)
    send_carried()
    wait(cotangents[0][0])
    wait(state["carried"])
    forward_x(0)
    (quads[1],) = small(stack_quad, [halves[0], rest_one], [((QUAD, 2 * PAIRS[1]), BF)], "stack_quad")
    rest_two = dp_permute(first(halves[1]), functools.partial(z_to, 2))
    wait(*far[0])
    send_x(1)
    back_work(0, 0)
    back_work(0, 1)
    (quads[2],) = small(stack_quad, [halves[1], rest_two], [((QUAD, 2 * PAIRS[2]), BF)], "stack_quad")
    send_cotangent(upstream_b, [1, 2])
    forward_x(1)
    reduce_first(0)
    wait(*far[1])
    send_x(2)
    send_incoming()
    back_work(1, 0)
    reduce_half(0)
    send_slot()
    back_work(1, 1)
    forward_x(2)
    wait(state["incoming"])
    reduce_first(1)
    back_work(2, 0)
    back_work(2, 1)
    finish()
    reduce_first(2)
    wait(state["slot"])
    send_half(0)
    forward_start()
    forward_work(0, 0)
    reduce_second(1)
    forward_work(0, 1)
    reduce_half(2)
    send_half(2)
    forward_work(1, 0)
    reduce_quarter(0)
    forward_work(1, 1)
    reduce_quarter(2)
    forward_work(2, 0)
    forward_work(2, 1)
    own_gain = lax.dynamic_slice_in_dim(gain, replica * 128, 128, axis=1)
    weight_sum, gain_sum = small(
        last_sums,
        [part for p in range(count_pairs) for part in sums[p]] + [shard, own_gain],
        [((128, D), F32), ((1, 128), F32)],
        "last_sums",
    )
    result, grad_input, memory_term = state["result"], state["dx"], state["dm"]
    return result[None], grad_input[None], memory_term[None], weight_sum[None], gain_sum


def forward_first(info, *refs):
    forward_chunk(info, *refs[:-2], None, *refs[-2:])


def solution(mesh):
    rows = P("section", "dp", None)
    one = P("section", "dp")
    return jax.shard_map(
        on_device,
        mesh=mesh,
        in_specs=(rows, rows, one, rows, rows, one, rows, rows, rows, P("section", None)),
        out_specs=(rows, rows, rows, rows, one),
        check_vma=False,
    )
```

```python
import functools

import jax
import jax.numpy as jnp
from jax import lax
from jax.experimental import pallas as pl
from jax.experimental.pallas import tpu as pltpu
from jax.sharding import PartitionSpec as P

HEADS = 32
HEAD = 64
D = 2048
ROWS = 256
BF = jnp.bfloat16
F32 = jnp.float32
PAIRS = (384, 384, 256)
CHUNKS = 2 * len(PAIRS)
QUAD = 512

epsilon = 1e-06
GELU_A = 0.7978845608028654
GELU_B = 0.044715

NT = (((1,), (1,)), ((), ()))


def dot(a, b):
    return jnp.dot(a, b, preferred_element_type=F32)


def dot_nt(a, b):
    return lax.dot_general(a, b, NT, preferred_element_type=F32)


def rows_loop(count, step, body):
    def run(index, carry):
        body(pl.ds(pl.multiple_of(index * step, step), step))
        return carry

    lax.fori_loop(0, count // step, run, 0)


def add(a, b):
    return (a.astype(F32) + b.astype(F32)).astype(BF)


def norm_rows(values):
    values = values.astype(F32)
    inverse = lax.rsqrt(jnp.mean(values * values, axis=-1, keepdims=True) + epsilon)
    return values * inverse, inverse


def prologue_back(info, x_ref, m_ref, g_ref, u_ref, ut_ref, k_ref):
    def body(rows):
        normed, _ = norm_rows(x_ref[rows, :])
        u_ref[rows, :] = (normed * g_ref[...]).astype(BF)

    rows_loop(ROWS, 32, body)

    @pl.when(info[0] == 1)
    def _():
        def keys(rows):
            k_ref[rows, :] = norm_rows(m_ref[rows, :])[0].astype(BF)

        rows_loop(ROWS, 32, keys)

    for index in range(D // 256):
        cols = slice(index * 256, index * 256 + 256)
        ut_ref[cols, :] = u_ref[:, cols].T


def prologue_forward(info, h_ref, s_ref, g_ref, u_ref, k_ref):
    first = info[1] == 1

    def body(rows):
        y = jnp.where(first, s_ref[rows, :].astype(F32), h_ref[rows, :].astype(F32))
        u_ref[rows, :] = (norm_rows(y)[0] * g_ref[...]).astype(BF)

    rows_loop(ROWS, 32, body)

    @pl.when(info[0] == 1)
    def _():
        def keys(rows):
            m = jnp.where(first, h_ref[rows, :].astype(F32), s_ref[rows, :].astype(F32))
            k_ref[rows, :] = norm_rows(m)[0].astype(BF)

        rows_loop(ROWS, 32, keys)


def gathered(info, source, quad):
    return jnp.concatenate([source[:, pl.ds(block_place(info, quad, i), 128)] for i in range(4)], axis=1)


def block_place(info, quad, index):
    return pl.multiple_of(info[4 + 4 * quad + index] * 128, 128)


def column_tiles(width):
    return [slice(start, min(start + 256, width)) for start in range(0, width, 256)]


def project(info, u_ref, parts, z_ref):
    width = z_ref.shape[1]
    for cols in column_tiles(width):
        total = None
        for quad, part in enumerate(parts):
            term = dot(gathered(info, u_ref, quad), part[:, cols])
            total = term if total is None else total + term
        z_ref[:, cols] = total


def lane_masks():
    lane = lax.broadcasted_iota(jnp.int32, (ROWS, 128), 1)
    return lane < HEAD, lane >= HEAD


def softmax_parts(scores, length):
    column = lax.broadcasted_iota(jnp.int32, scores.shape, 1).astype(F32)
    scores = jnp.where(column < length, scores, -1e30)
    top = jnp.max(scores, axis=-1, keepdims=True)
    raised = jnp.exp(scores - top)
    return raised * (1.0 / jnp.sum(raised, axis=-1, keepdims=True))


def back_chunk(info, u_ref, ut_ref, w0, w1, w2, w3, c_ref, k_ref, v_ref, dz_ref, d0, d1, d2, d3, dk_ref, dv_ref, z_ref):
    project(info, u_ref, (w0, w1, w2, w3), z_ref)

    @pl.when(info[0] == 0)
    def _():
        def body(rows):
            z = z_ref[rows, :]
            square = z * z
            t = jnp.tanh(GELU_A * (z + GELU_B * (square * z)))
            slope = 0.5 * (1.0 + t) + (0.5 * GELU_A) * z * (1.0 - t * t) * (1.0 + (3 * GELU_B) * square)
            dz_ref[rows, :] = (c_ref[rows, :].astype(F32) * slope).astype(BF)

        rows_loop(ROWS, 32, body)

    @pl.when(info[0] == 1)
    def _():
        length = info[2].astype(F32)

        def pair(index, carry):
            cols = pl.ds(pl.multiple_of(index * 128, 128), 128)
            q = z_ref[:, cols].astype(BF)
            k = k_ref[:, cols]
            v = v_ref[:, cols]
            do = c_ref[:, cols]
            qt = q.T
            dot_t = do.T
            q_small = (q.astype(F32) * 0.125).astype(BF)
            do_small = (do.astype(F32) * 0.125).astype(BF)
            zero = jnp.zeros((), BF)
            total = None
            dks, dvs = [], []
            for head, mask in enumerate(lane_masks()):
                p = softmax_parts(dot_nt(jnp.where(mask, q_small, zero), k), length)
                dp = dot_nt(jnp.where(mask, do_small, zero), v)
                shift = jnp.sum(dp * p, axis=-1, keepdims=True)
                ds = (p * (dp - shift)).astype(BF)
                pb = p.astype(BF)
                term = dot(ds, jnp.where(mask, k, zero))
                total = term if total is None else total + term
                rows = slice(head * HEAD, head * HEAD + HEAD)
                dks.append(dot(qt[rows, :], ds))
                dvs.append(dot(dot_t[rows, :], pb))
            dz_ref[:, cols] = total.astype(BF)
            dk_ref[:, cols] = jnp.concatenate(dks, axis=0).T
            dv_ref[:, cols] = jnp.concatenate(dvs, axis=0).T
            return carry

        lax.fori_loop(0, z_ref.shape[1] // 128, pair, 0)

    for quad, out in enumerate((d0, d1, d2, d3)):
        ut = jnp.concatenate([ut_ref[pl.ds(block_place(info, quad, i), 128), :] for i in range(4)], axis=0)
        for cols in column_tiles(z_ref.shape[1]):
            out[:, cols] = dot(ut, dz_ref[:, cols]).astype(BF)


def forward_chunk(info, u_ref, w0, w1, w2, w3, h_ref, m_ref, k_ref, n_ref, old_ref, out_ref, z_ref):
    project(info, u_ref, (w0, w1, w2, w3), z_ref)

    @pl.when(info[0] == 0)
    def _():
        def body(rows):
            z = z_ref[rows, :]
            t = jnp.tanh(GELU_A * (z + GELU_B * (z * z * z)))
            out_ref[rows, :] = (h_ref[rows, :].astype(F32) + 0.5 * z * (1.0 + t)).astype(BF)

        rows_loop(ROWS, 32, body)

    @pl.when(info[0] == 1)
    def _():
        length = n_ref[...].astype(F32)[:1, :1]
        first = info[1] == 1

        def pair(index, carry):
            cols = pl.ds(pl.multiple_of(index * 128, 128), 128)
            q = (z_ref[:, cols].astype(BF).astype(F32) * 0.125).astype(BF)
            k = k_ref[:, cols]
            h = h_ref[:, cols].astype(F32)
            m = m_ref[:, cols].astype(F32)
            y = jnp.where(first, m, h)
            v = jnp.where(first, h, m).astype(BF)
            zero = jnp.zeros((), BF)
            total = y
            for mask in lane_masks():
                p = softmax_parts(dot_nt(jnp.where(mask, q, zero), k), length)
                total = total + dot(p.astype(BF), jnp.where(mask, v, zero))
            out_ref[:, cols] = total.astype(BF)
            return carry

        lax.fori_loop(0, z_ref.shape[1] // 128, pair, 0)


def epilogue(info, *refs):
    dzs, refs = refs[:CHUNKS], refs[CHUNKS:]
    parts, refs = refs[: 4 * CHUNKS], refs[4 * CHUNKS :]
    dks, refs = refs[:CHUNKS], refs[CHUNKS:]
    dvs, refs = refs[:CHUNKS], refs[CHUNKS:]
    cs, refs = refs[:2], refs[2:]
    x_ref, m_ref, a_ref, g_ref, dx_ref, dm_ref, du_ref = refs
    for quad in range(4):
        total = None
        for chunk in range(CHUNKS):
            term = dot_nt(dzs[chunk][...], parts[4 * chunk + quad][...])
            total = term if total is None else total + term
        for index in range(4):
            du_ref[:, pl.ds(block_place(info, quad, index), 128)] = total[:, index * 128 : index * 128 + 128]

    def body(rows):
        normed, inverse = norm_rows(x_ref[rows, :])
        du = du_ref[rows, :]
        h = du * g_ref[...]
        mean = jnp.mean(h * normed, axis=-1, keepdims=True)
        c = jnp.concatenate([ref[rows, :] for ref in cs], axis=1).astype(F32)
        dx_ref[rows, :] = (c + inverse * h - normed * (inverse * mean)).astype(BF)

    rows_loop(ROWS, 32, body)

    @pl.when(info[0] == 0)
    def _():
        dm_ref[...] = jnp.zeros_like(dm_ref)

    @pl.when(info[0] == 1)
    def _():
        def back(rows):
            normed, inverse = norm_rows(m_ref[rows, :])
            dk = jnp.concatenate([ref[rows, :] for ref in dks], axis=1)
            dv = jnp.concatenate([ref[rows, :] for ref in dvs], axis=1)
            mean = jnp.mean(dk * normed, axis=-1, keepdims=True)
            dm_ref[rows, :] = dv + inverse * dk - normed * (inverse * mean) + a_ref[rows, :].astype(F32)

        rows_loop(ROWS, 32, back)


def extend_rows(info, value, out):
    out[:ROWS, :] = value[...]
    out[ROWS:, :] = jnp.full((16, D), info[3].astype(F32), F32).astype(BF)


def split_columns(info, value, *outs):
    start = 0
    for out in outs:
        out[...] = value[:, start : start + out.shape[1]]
        start += out.shape[1]


def cotangent_kernel(info, p_ref, g_ref, up0, up1, pb_ref):
    first = info[1] == 1

    def body(rows):
        p = p_ref[rows, :]
        pb_ref[rows, :] = p.astype(BF)
        up = jnp.where(first, p, g_ref[rows, :].astype(F32)).astype(BF)
        up0[rows, :] = up[:, : up0.shape[1]]
        up1[rows, :] = up[:, up0.shape[1] :]

    rows_loop(ROWS, 32, body)


def stack_rows(info, *refs):
    parts, outs = refs[:4], refs[4:]
    for index, part in enumerate(parts):
        start = 0
        for out in outs:
            out[index * 128 : index * 128 + 128, :] = part[:, start : start + out.shape[1]]
            start += out.shape[1]


def stack_two(info, one, two, *outs):
    start = 0
    for out in outs:
        cols = slice(start, start + out.shape[1])
        out[:128, :] = one[:, cols]
        out[128:, :] = two[:, cols]
        start += out.shape[1]


def stack_quad(info, one, two, out):
    out[:256, :] = one[...]
    out[256:, :] = two[...]


def take_two(info, one, two, out_one, out_two):
    out_one[...] = one[...]
    out_two[...] = two[...]


def first_sums(info, q1a, sa, q1b, q2a, q2b, sb, one, two):
    width = q1a.shape[1]
    one[:, :width] = add(q1a[...], sa[...])
    one[:, width:] = q1b[...]
    two[:, :width] = q2a[...]
    two[:, width:] = add(q2b[...], sb[...])


def second_sums(info, own_a, own_b, t1, t2, keep, s1, s2, s3):
    width = own_a.shape[1]
    for index, out in enumerate((keep, s1, s2, s3)):
        rows = slice(index * 128, index * 128 + 128)
        for own, cols in ((own_a, slice(0, width)), (own_b, slice(width, 2 * width))):
            total = own[rows, :].astype(F32) + t1[rows, cols].astype(F32) + t2[rows, cols].astype(F32)
            out[:, cols] = total.astype(out.dtype)


def half_sums(info, own_a, own_b, t1, t2, keep, sent):
    width = own_a.shape[1]
    for own, cols in ((own_a, slice(0, width)), (own_b, slice(width, 2 * width))):
        total = own[...].astype(F32) + t1[:, cols].astype(F32) + t2[:, cols].astype(F32)
        keep[:, cols] = total[:256]
        sent[:, cols] = total[256:].astype(BF)


def quarter_sums(info, kept, came, keep, sent):
    total = kept[...] + came[...].astype(F32)
    keep[...] = total[:128]
    sent[...] = total[128:].astype(BF)


def last_sums(info, *refs):
    w_ref, g_ref, out_ref, gain_ref = refs[-4:]
    total = None
    start = 0
    for p in range(len(PAIRS)):
        some = 4 if p == 1 else 2
        (keep, *came), refs = refs[:some], refs[some:]
        value = keep[...]
        for part in came:
            value += part[...].astype(F32)
        cols = slice(start, start + keep.shape[1])
        start += keep.shape[1]
        out_ref[:, cols] = value
        term = jnp.sum(value * w_ref[:, cols].astype(F32), axis=1, keepdims=True)
        total = term if total is None else total + term
    gain_ref[...] = jnp.broadcast_to(total, (128, 128)).T[0:1, :] / g_ref[...]


def call(body, info, ins, outs, scratch=(), aliases=None, flops=1, limit=10, name=None):
    def spec(shape, block):
        if block == -1:
            return pl.BlockSpec(memory_space=pl.ANY)
        if block == "length":
            return pl.BlockSpec((16, 128), lambda step, info: (ROWS // 16, 0))
        if block == "rows":
            return pl.BlockSpec((ROWS, D), lambda step, info: (0, 0))
        if block is None:
            return pl.BlockSpec(shape, lambda step, info: (0,) * len(shape))
        start, width = block
        return pl.BlockSpec((ROWS if shape[0] == ROWS + 16 else shape[0], width), lambda step, info: (0, start // width))

    return pl.pallas_call(
        body,
        grid_spec=pltpu.PrefetchScalarGridSpec(
            num_scalar_prefetch=1,
            grid=(1,),
            in_specs=[spec(a.shape, b) for a, b in ins],
            out_specs=[spec(s, b) for s, _, b in outs],
            scratch_shapes=list(scratch),
        ),
        out_shape=[jax.ShapeDtypeStruct(s, t) for s, t, _ in outs],
        input_output_aliases=aliases or {},
        compiler_params=pltpu.CompilerParams(vmem_limit_bytes=limit * 2**20),
        cost_estimate=pl.CostEstimate(flops=flops, bytes_accessed=1, transcendentals=0),
        name=name,
    )(info, *[a for a, _ in ins])


def dp_permute(value, step):
    pairs = []
    for x in range(4):
        for z in range(4):
            to = step(x, z)
            if to is not None:
                pairs.append((x * 4 + z, to[0] * 4 + to[1]))
    return lax.ppermute(value, "dp", pairs)


def z_steps(value):
    return [dp_permute(value, functools.partial(z_to, step)) for step in (1, 2, 3)]


def z_two(total):
    return dp_permute(total, functools.partial(z_to, 2))


def z_to(step, x, z):
    return (x, z ^ step)


def x_swap(x, z):
    return (x ^ 1, z)


def x_cross(x, z):
    return (3 - x, z)


def tie(value, *after):
    return lax.optimization_barrier((value, *after))[0] if after else value


def on_device(
    handoff,
    memory_slot,
    memory_length,
    saved_input,
    saved_memory,
    saved_length,
    grad_handoff,
    memory_grad_partial,
    section_weight,
    section_gain,
):
    section = lax.axis_index("section")
    replica = lax.axis_index("dp")
    count = lax.axis_size("section")
    half = count // 2
    x, z = replica // 4, replica % 4
    gain = section_gain
    shard = section_weight[0]

    def along(value, pairs):
        return lax.ppermute(value, "section", pairs)

    starts = [0]
    for width in PAIRS:
        starts.append(starts[-1] + 2 * width)
    blocks = [(starts[i] + h * w, w) for i, w in enumerate(PAIRS) for h in (0, 1)]
    marks = []

    def first(value):
        return tie(value, *marks)

    def mark(value):
        marks[:] = [value]
        return value

    count_pairs = len(PAIRS)
    quads, near, far = {}, {}, {}
    is_decoder = (section >= half).astype(jnp.int32)
    is_first = (section == half).astype(jnp.int32)
    order = [(x ^ i) * 4 + (z ^ j) for i in (0, 1, 3, 2) for j in range(4)]

    lengths = [saved_length[0, 0], memory_length[0, 0]]
    info = jnp.stack([v.astype(jnp.int32) for v in [is_decoder, is_first] + lengths + order])

    def small(body, ins, shapes, name):
        ins = [i if isinstance(i, tuple) else (i, None) for i in ins]
        ins[0] = (first(ins[0][0]), ins[0][1])
        out = call(body, info, ins, [(*shape, None) for shape in shapes], name=name)
        mark(out[0])
        return out

    head = 2 * PAIRS[0]
    columns = ((128, head), BF), ((128, D - head), BF)
    shard_a, shard_b = small(split_columns, [shard], columns, "split")
    came_a = z_steps(shard_a)
    swapped_b = dp_permute(shard_b, functools.partial(z_to, 1))
    upstream_a, upstream_b, partial = small(
        cotangent_kernel,
        [memory_grad_partial[0], grad_handoff[0]],
        [((ROWS, head), BF), ((ROWS, D - head), BF), ((ROWS, D), BF)],
        "cotangent",
    )
    cotangents = {}

    def send_cotangent(part, pairs):
        part = along(first(part), [(s, (s - 1) % count) for s in range(count)])
        for index in pairs:
            cotangents[index] = (part, starts[index] - starts[pairs[0]])

    def send_x(p):
        sent = first(quads[p])
        near[p] = (dp_permute(sent, x_swap), dp_permute(sent, x_cross))

    def forward_x(p):
        w = PAIRS[p]
        one, two = small(take_two, [(near[p][0], (0, w)), (near[p][1], (w, w))], [((QUAD, w), BF)] * 2, "forward")
        far[p] = (dp_permute(one, x_cross), dp_permute(two, x_swap))

    def weights(p, kind):
        w = PAIRS[p]
        return [(a, (kind * w, w)) for a in (quads[p], *near[p])] + [(far[p][kind], None)]

    whole = lambda t: ((ROWS, D), t, None)
    u_back, ut_back, k_back = call(
        prologue_back,
        info,
        [(first(saved_input[0]), None), (saved_memory[0], None), (gain, None)],
        [whole(BF), ((D, ROWS), BF, None), whole(BF)],
        name="prologue_back",
    )
    mark(u_back)
    back, back_terms, sums = {}, {}, {}

    def back_work(p, kind):
        index = 2 * p + kind
        start, width = blocks[index]
        part = ((ROWS, width), F32, None)
        rows = ((QUAD, width), BF, None)
        out = call(
            back_chunk,
            info,
            [(first(u_back), None), (ut_back, None)]
            + weights(p, kind)
            + [(cotangents[p][0], (cotangents[p][1] + kind * width, width))]
            + [(a, blocks[index]) for a in (k_back, saved_memory[0])],
            [((ROWS, width), BF, None), rows, rows, rows, rows, part, part],
            scratch=[pltpu.VMEM((ROWS, width), F32)],
            name="back_chunk",
        )
        mark(out[0])
        back[index] = (out[0], out[5], out[6])
        back_terms[index] = list(out[1:5]) + [dp_permute(out[4], x_swap if kind else x_cross)]

    def reduce_first(p):
        a, b = back_terms[2 * p], back_terms[2 * p + 1]
        shape = ((QUAD, 2 * PAIRS[p]), BF)
        one, two = small(first_sums, [a[1], a[4], b[1], a[2], b[2], b[4]], [shape, shape], "first_sums")
        sums[p] = (dp_permute(one, x_swap), dp_permute(two, x_cross))

    def reduce_second(p):
        width = 2 * PAIRS[p]
        shapes = [((128, width), F32)] + [((128, width), BF)] * 3
        own = [back_terms[2 * p][0], back_terms[2 * p + 1][0]]
        keep, *sent = small(second_sums, own + list(sums[p]), shapes, "second_sums")
        sums[p] = [keep] + [dp_permute(part, functools.partial(z_to, i + 1)) for i, part in enumerate(sent)]

    def reduce_half(p):
        width = 2 * PAIRS[p]
        own = [back_terms[2 * p][0], back_terms[2 * p + 1][0]]
        sums[p] = small(half_sums, own + list(sums[p]), [((256, width), F32), ((256, width), BF)], "half_sums")

    def send_half(p):
        sums[p] = [sums[p][0], z_two(first(sums[p][1]))]

    def reduce_quarter(p):
        width = 2 * PAIRS[p]
        keep, sent = small(quarter_sums, sums[p], [((128, width), F32), ((128, width), BF)], "quarter_sums")
        sums[p] = [keep, dp_permute(sent, functools.partial(z_to, 1))]

    state = {}

    def send_incoming():
        state["incoming"] = along(first(handoff[0]), [(s, (s + 1) % count) for s in range(count)])

    def make_slot():
        (state["extended"],) = small(extend_rows, [memory_slot[0]], [((ROWS + 16, D), BF)], "extend")

    def send_slot():
        state["slot"] = along(first(state["extended"]), [(s, s + 1) for s in range(half - 1, count - 1)])

    def send_carried():
        state["carried"] = along(first(partial), [(s, s - 1) for s in range(half + 1, count)])

    def wait(*values):
        marks.extend(values)

    def forward_start():
        state["u"], state["k"] = call(
            prologue_forward,
            info,
            [(first(state["incoming"]), None), (state["slot"], "rows"), (gain, None)],
            [whole(BF), whole(BF)],
            name="prologue_forward",
        )
        mark(state["u"])

    def forward_work(p, kind):
        index = 2 * p + kind
        old = [(state["result"], -1)] if "result" in state else []
        (state["result"],) = call(
            forward_chunk if old else forward_first,
            info,
            [(first(state["u"]), None)]
            + weights(p, kind)
            + [(a, blocks[index]) for a in (state["incoming"], state["slot"], state["k"])]
            + [(state["slot"], "length")]
            + old,
            [((ROWS, D), BF, blocks[index])],
            scratch=[pltpu.VMEM((ROWS, blocks[index][1]), F32)],
            aliases={10: 0} if old else None,
            name="forward_chunk",
        )
        mark(state["result"])

    def finish():
        kinds = [(p, k) for p in range(count_pairs) for k in (0, 1)]
        state["dx"], state["dm"] = call(
            epilogue,
            info,
            [(first(back[0][0]), None)]
            + [(back[i][0], None) for i in range(1, CHUNKS)]
            + [part for p, k in kinds for part in weights(p, k)]
            + [(back[i][1], None) for i in range(CHUNKS)]
            + [(back[i][2], None) for i in range(CHUNKS)]
            + [(cotangents[0][0], None), (cotangents[1][0], None)]
            + [(saved_input[0], None), (saved_memory[0], None), (state["carried"], None), (gain, None)],
            [whole(BF), whole(F32)],
            scratch=[pltpu.VMEM((ROWS, D), F32)],
            limit=30,
            name="epilogue",
        )
        mark(state["dx"])

    send_cotangent(upstream_a, [0])
    make_slot()
    halves = small(stack_two, [shard_b, swapped_b], [((256, 2 * w), BF) for w in PAIRS[1:]], "stack_two")
    rest_one = dp_permute(halves[0], functools.partial(z_to, 2))
    (quads[0],) = small(stack_rows, [shard_a] + came_a, [((QUAD, head), BF)], "stack")
    send_x(0)
    send_carried()
    wait(cotangents[0][0])
    wait(state["carried"])
    forward_x(0)
    (quads[1],) = small(stack_quad, [halves[0], rest_one], [((QUAD, 2 * PAIRS[1]), BF)], "stack_quad")
    rest_two = dp_permute(first(halves[1]), functools.partial(z_to, 2))
    wait(*far[0])
    send_x(1)
    back_work(0, 0)
    back_work(0, 1)
    (quads[2],) = small(stack_quad, [halves[1], rest_two], [((QUAD, 2 * PAIRS[2]), BF)], "stack_quad")
    send_cotangent(upstream_b, [1, 2])
    forward_x(1)
    reduce_first(0)
    wait(*far[1])
    send_x(2)
    send_incoming()
    back_work(1, 0)
    back_work(1, 1)
    reduce_half(0)
    send_slot()
    forward_x(2)
    wait(state["incoming"])
    reduce_first(1)
    back_work(2, 0)
    back_work(2, 1)
    finish()
    reduce_first(2)
    wait(state["slot"])
    send_half(0)
    forward_start()
    forward_work(0, 0)
    reduce_second(1)
    forward_work(0, 1)
    reduce_half(2)
    send_half(2)
    forward_work(1, 0)
    reduce_quarter(0)
    forward_work(1, 1)
    reduce_quarter(2)
    forward_work(2, 0)
    forward_work(2, 1)
    own_gain = lax.dynamic_slice_in_dim(gain, replica * 128, 128, axis=1)
    weight_sum, gain_sum = small(
        last_sums,
        [part for p in range(count_pairs) for part in sums[p]] + [shard, own_gain],
        [((128, D), F32), ((1, 128), F32)],
        "last_sums",
    )
    result, grad_input, memory_term = state["result"], state["dx"], state["dm"]
    return result[None], grad_input[None], memory_term[None], weight_sum[None], gain_sum


def forward_first(info, *refs):
    forward_chunk(info, *refs[:-2], None, *refs[-2:])


def solution(mesh):
    rows = P("section", "dp", None)
    one = P("section", "dp")
    return jax.shard_map(
        on_device,
        mesh=mesh,
        in_specs=(rows, rows, one, rows, rows, one, rows, rows, rows, P("section", None)),
        out_specs=(rows, rows, rows, rows, one),
        check_vma=False,
    )
```
